32 devices in a mesh: fx: 4 (over z), fy: 8 (over y, x, core).
Axes of the slice: x: 2, y: 2, z: 4, core: 2. Of those that a mesh axis runs over, the one named last changes fastest.
Arguments:
- tracers: float32 [4, 60, 512, 512], P(None, None, 'fy', 'fx'), may hold values from -6 to 6
- stream: float32 [60, 512, 512], P(None, 'fy', 'fx'), may hold values from -0.45 to 0.45
- land_mask: int32 [512, 512], P('fy', 'fx'), may hold values 0 or 1
- convect_mask: int32 [512, 512], P('fy', 'fx'), may hold values from 0 to 1, as said below
- regime_label: int32 [512, 512], P('fy', 'fx'), may hold values from 0 to 3
- w_in: bfloat16 [512, 241], replicated, may hold values from -0.25 to 0.25
- w_hid: bfloat16 [6, 512, 512], replicated, may hold values from -0.375 to 0.375
- b_hid: float32 [7, 512], replicated, may hold values from -1.5 to 1.5
- w_out: bfloat16 [244, 512], replicated, may hold values from -0.25 to 0.25
- b_out: float32 [244], replicated, may hold values from -2.5 to 2.5
Outputs:
- new_state: float32 [4, 60, 512, 512], P(None, None, 'fy', 'fx')
- regime_loss: float32 [512, 512], P('fy', 'fx')
The draws below stay inside these ranges and needn't reach their ends.
Inputs may be any that keep to these rules, and one draw needn't show every extreme that they name: `convect_mask`: the face splits into blocks of 64 x 128 cells (one per device). In every strip of blocks that share their cells along the second dimension, exactly one block, drawn at random, holds exactly 4096 active columns and every other block exactly 1024; so every strip holds exactly 11264. Positions within a block are random.
All inputs are finite; a program needn't handle non-finite values. No bound on the sum of `land_mask` on one device may be relied on, other than what follows from the above.
Results may differ from the reference program's by a relative error of at most 0.0026.
Values may be sent and summed in bfloat16 or wider, within the bound.
A program may use at most 192 MiB of HBM per device.

```python
import jax
import jax.numpy as jnp

CY = 64
CX = 128
LEV = 60
NV = 4
SUBSTEPS = 4
H = 512
NH = 6
K = 4
F_IN = 241
OUTS = 244
CAP = 4096
LOW = 1024
NY = 512
NX = 512
N_FX = 4
N_FY = 8


def draw_convect_mask(key, part):
    block = CY * CX
    key_hot = jax.random.fold_in(key, 11)
    key_score = jax.random.fold_in(key, 23)
    hottest = jax.random.randint(key_hot, (1, N_FX, 1), 0, N_FY)
    strips = jnp.arange(N_FY).reshape(N_FY, 1, 1)
    wanted = jnp.where(strips == hottest, CAP, LOW)
    upper = 2 ** 30 // block
    scores = jax.random.randint(key_score, (N_FY, N_FX, block), 0, upper) * block + jnp.arange(block).reshape(1, 1, block)
    ranks = jnp.argsort(jnp.argsort(scores, axis=-1), axis=-1)
    active = (ranks < wanted).astype(jnp.int32)
    return active.reshape(N_FY, N_FX, CY, CX).transpose(0, 2, 1, 3).reshape(NY, NX)


def draw_tracers(key, part):
    key_value = jax.random.fold_in(key, 31)
    rows = jnp.arange(NY) % CY
    cols = jnp.arange(NX) % CX
    row_edge = jnp.minimum(rows, CY - 1 - rows)
    col_edge = jnp.minimum(cols, CX - 1 - cols)
    near = jnp.minimum(row_edge[:, None], col_edge[None, :]) < SUBSTEPS
    weight = jnp.where(near, 1.0, 0.05).astype(jnp.float32)
    rough = jax.random.uniform(key_value, (NV, LEV, NY, NX), jnp.float32, -6.0, 6.0)
    return (rough * weight).astype(jnp.float32)


def draw_stream(key, part):
    key_sign = jax.random.fold_in(key, 41)
    key_size = jax.random.fold_in(key, 43)
    signs = jax.random.rademacher(key_sign, (LEV, NY, NX)).astype(jnp.float32)
    magnitude = jax.random.uniform(key_size, (LEV, NY, NX), jnp.float32, 0.3, 0.45)
    return (signs * magnitude).astype(jnp.float32)


def plant(values, own_key, low, top_value):
    dims = values.shape
    spot = [jax.random.randint(jax.random.fold_in(own_key, axis), (), 0, dims[axis]) for axis in range(len(dims))]
    values = values.at[tuple(spot)].set(low)
    longest = dims.index(max(dims))
    spot[longest] = (spot[longest] + 1) % dims[longest]
    return values.at[tuple(spot)].set(top_value)


def normal_values(rng, dims, spread, most, held_as=jnp.bfloat16):
    return jnp.clip(spread * jax.random.normal(rng, dims, jnp.float32), -most, most).astype(held_as)


def setup_inputs(seed: int = 0) -> dict:
    splits = jax.random.split(jax.random.key(seed), 11)
    return {
        "tracers": draw_tracers(jax.random.fold_in(splits[10], 71), 0),
        "stream": draw_stream(jax.random.fold_in(splits[10], 71), 0),
        "land_mask": plant((jax.random.randint(splits[2], (NY, NX), 0, 10) < 3).astype(jnp.int32), jax.random.fold_in(splits[2], 1), 0, 1),
        "convect_mask": draw_convect_mask(jax.random.fold_in(splits[10], 71), 0),
        "regime_label": plant(jax.random.randint(splits[4], (NY, NX), 0, K), jax.random.fold_in(splits[4], 1), 0, K - 1).astype(jnp.int32),
        "w_in": normal_values(splits[5], (H, F_IN), (2 * F_IN) ** -0.5, 0.25),
        "w_hid": normal_values(splits[6], (NH, H, H), (H // 2) ** -0.5, 0.375),
        "b_hid": normal_values(splits[7], (NH + 1, H), 0.3, 1.5, jnp.float32),
        "w_out": normal_values(splits[8], (OUTS, H), H ** -0.5, 0.25),
        "b_out": normal_values(splits[9], (OUTS,), 0.5, 2.5, jnp.float32),
    }


def face_speeds(padded):
    corner = (padded[:, :-1, :-1] + padded[:, :-1, 1:] + padded[:, 1:, :-1] + padded[:, 1:, 1:]) * 0.25
    east_speed = -(corner[:, 1:, :] - corner[:, :-1, :])
    north_speed = corner[:, :, 1:] - corner[:, :, :-1]
    return east_speed, north_speed


def transport(padded, east_speed, north_speed):
    flux_east = jnp.maximum(east_speed, 0.0) * padded[:, :, 1:-1, :-1] + jnp.minimum(east_speed, 0.0) * padded[:, :, 1:-1, 1:]
    flux_north = jnp.maximum(north_speed, 0.0) * padded[:, :, :-1, 1:-1] + jnp.minimum(north_speed, 0.0) * padded[:, :, 1:, 1:-1]
    centre = padded[:, :, 1:-1, 1:-1]
    return centre - (flux_east[..., 1:] - flux_east[..., :-1]) - (flux_north[:, :, 1:, :] - flux_north[:, :, :-1, :])


def run_network(inputs, w_in, w_hid, b_hid, w_out, b_out):
    hidden = jax.nn.leaky_relu(jnp.dot(w_in, inputs, preferred_element_type=jnp.float32) + b_hid[0][:, None], negative_slope=0.15).astype(jnp.bfloat16)
    for hidden_index in range(w_hid.shape[0]):
        summed = jnp.dot(w_hid[hidden_index], hidden, preferred_element_type=jnp.float32) + b_hid[hidden_index + 1][:, None]
        hidden = jax.nn.leaky_relu(summed, negative_slope=0.15).astype(jnp.bfloat16)
    return (jnp.dot(w_out, hidden, preferred_element_type=jnp.float32) + b_out[:, None]).astype(jnp.bfloat16)


def reference(tracers, stream, land_mask, convect_mask, regime_label, w_in, w_hid, b_hid, w_out, b_out):
    east_speed, north_speed = face_speeds(jnp.pad(stream, ((0, 0), (1, 1), (1, 1))))
    field = tracers
    for substep in range(SUBSTEPS):
        field = transport(jnp.pad(field, ((0, 0), (0, 0), (1, 1), (1, 1))), east_speed, north_speed)
    columns = NY * NX
    flat_state = field.reshape(NV * LEV, columns)
    land_row = 4.0 * land_mask.reshape(1, columns).astype(jnp.float32)
    features = jnp.concatenate([flat_state, land_row], axis=0).astype(jnp.bfloat16)
    flat_active = convect_mask.reshape(columns)
    total = N_FX * (CAP + (N_FY - 1) * LOW)
    chosen = jnp.nonzero(flat_active, size=total, fill_value=0)[0].astype(jnp.int32)
    result = run_network(features[:, chosen], w_in, w_hid, b_hid, w_out, b_out)
    per_cell = jnp.zeros((NV * LEV + K, columns), jnp.bfloat16).at[:, chosen].set(result)
    active = flat_active.astype(jnp.float32)
    tendency = per_cell[:NV * LEV].astype(jnp.float32) * active[None, :]
    new_state = (flat_state + tendency).reshape(NV, LEV, NY, NX)
    evidence = per_cell[NV * LEV:].astype(jnp.float32)
    alpha = 1.0 + jax.nn.softplus(evidence)
    strength = jnp.sum(alpha, axis=0)
    labels = regime_label.reshape(1, columns)
    picked = jnp.sum(jnp.where(labels == jnp.arange(K).reshape(K, 1), alpha, 0.0), axis=0)
    loss = active * (jnp.log(strength) - jnp.log(picked))
    return new_state, loss.reshape(NY, NX)
```

```python
import functools

import jax
import jax.numpy as jnp
from jax import lax
from jax.experimental import pallas as pl
from jax.experimental.pallas import tpu as pltpu
from jax.sharding import PartitionSpec as P

SUBSTEPS = 4
MESH = pl.DeviceIdType.MESH
CHUNK = 256
WINDOW = 384
TILE = 1024
MOST = 4096
GROUP = 6
STEP = 20

WAYS = ((-1, 0), (1, 0), (0, 1), (0, -1), (-1, 1), (1, 1), (-1, -1), (1, -1))


def halo_kernel(
    n_fy,
    n_fx,
    tr_hbm,
    st_hbm,
    row_out,
    col_out,
    fields,
    row_send,
    row_recv,
    col_send,
    col_recv,
    corner_send,
    corner_recv,
    load_sem,
    send_sem,
    recv_sem,
):
    y = lax.axis_index("fy")
    x = lax.axis_index("fx")
    levels = st_hbm.shape[0]
    per = 2 * GROUP
    parts = levels // per

    def inside(dy, dx):
        ok_y = (y + dy >= 0) & (y + dy < n_fy)
        ok_x = (x + dx >= 0) & (x + dx < n_fx)
        return ok_y & ok_x

    barrier = pltpu.get_barrier_semaphore()
    for dy, dx in WAYS:

        @pl.when(inside(dy, dx))
        def _():
            pl.semaphore_signal(barrier, inc=1, device_id=(x + dx, y + dy), device_id_type=MESH)

    def loads(part):
        span = pl.ds(part * per, per)
        return (
            pltpu.make_async_copy(
                tr_hbm.at[:, span], fields.at[pl.ds(0, 4), span], load_sem.at[0, part]
            ),
            pltpu.make_async_copy(st_hbm.at[span], fields.at[4, span], load_sem.at[1, part]),
        )

    for part in range(parts):
        for copy in loads(part):
            copy.start()

    lane = lax.broadcasted_iota(jnp.int32, (64, 128), 1)
    low = lax.broadcasted_iota(jnp.int32, (8, 128), 0) < 4

    @pl.loop(0, parts)
    def _(part):
        for copy in loads(part):
            copy.wait()
        first = part * per
        for half in range(2):
            east = jnp.zeros((64, 128), jnp.float32)
            west = jnp.zeros((64, 128), jnp.float32)
            for k in range(GROUP):
                for f in range(5):
                    cells = fields[f, first + half * GROUP + k]
                    at = k * STEP + f * 4
                    mask = (lane >= at) & (lane < at + 4)
                    east = jnp.where(mask, pltpu.roll(cells, (at - 124) % 128, 1), east)
                    west = jnp.where(mask, pltpu.roll(cells, at, 1) if at else cells, west)
            for d, packed in enumerate((east, west)):
                col_send[d, part * 2 + half] = packed.astype(jnp.bfloat16)
                ends = jnp.where(low, packed[0:8], packed[56:64])
                corner_send[d, part * 2 + half] = jnp.concatenate(
                    [ends, jnp.zeros_like(ends)], axis=0
                ).astype(jnp.bfloat16)
        for quad in range(per // 4):
            for f in range(5):
                heads = [fields[f, first + quad * 4 + j, 0:8] for j in range(4)]
                tails = [fields[f, first + quad * 4 + j, 56:64] for j in range(4)]
                up = [
                    jnp.where(low, heads[j], pltpu.roll(heads[j + 1], 4, 0)) for j in (0, 2)
                ]
                down = [
                    jnp.where(low, pltpu.roll(tails[j], 4, 0), tails[j + 1]) for j in (0, 2)
                ]
                row_send[0, f, part * 3 + quad] = jnp.concatenate(up, 0).astype(jnp.bfloat16)
                row_send[1, f, part * 3 + quad] = jnp.concatenate(down, 0).astype(jnp.bfloat16)

    tall = 1 + (y > 0).astype(jnp.int32) + (y < n_fy - 1).astype(jnp.int32)
    wide = 1 + (x > 0).astype(jnp.int32) + (x < n_fx - 1).astype(jnp.int32)
    pl.semaphore_wait(barrier, tall * wide - 1)

    def copies():
        for way, (dy, dx) in enumerate(WAYS):
            if way < 2:
                src, dst = row_send.at[way], row_recv.at[way]
            elif way < 4:
                src, dst = col_send.at[way - 2], col_recv.at[way - 2]
            else:
                src, dst = corner_send.at[(way - 4) // 2], corner_recv.at[way - 4]
            yield way, dy, dx, src, dst, pltpu.make_async_remote_copy(
                src_ref=src,
                dst_ref=dst,
                send_sem=send_sem.at[way],
                recv_sem=recv_sem.at[way],
                device_id=(x + dx, y + dy),
                device_id_type=MESH,
            )

    for way, dy, dx, src, dst, copy in copies():

        @pl.when(inside(dy, dx))
        def _():
            copy.start()

    for way, dy, dx, src, dst, copy in copies():

        @pl.when(inside(-dy, -dx))
        def _():
            copy.wait_recv()

        @pl.when(jnp.logical_not(inside(-dy, -dx)))
        def _():
            dst[...] = jnp.zeros(dst.shape, dst.dtype)

    @pl.loop(0, levels // 4)
    def _(quad):
        for f in range(5):
            below = row_recv[0, f, quad].astype(jnp.float32)
            above = row_recv[1, f, quad].astype(jnp.float32)
            for j in range(4):
                b = below[8 * (j // 2) : 8 * (j // 2) + 8]
                a = above[8 * (j // 2) : 8 * (j // 2) + 8]
                if j % 2:
                    b = pltpu.roll(b, 4, 0)
                else:
                    a = pltpu.roll(a, 4, 0)
                row_out[f, quad * 4 + j] = jnp.where(low, b, a)

    @pl.loop(0, levels // GROUP)
    def _(group):
        for d in range(2):
            col_out[d, group, 0:64] = col_recv[d, group].astype(jnp.float32)
            below = corner_recv[2 * d, group].astype(jnp.float32)[0:8]
            above = corner_recv[2 * d + 1, group].astype(jnp.float32)[0:8]
            col_out[d, group, 64:72] = jnp.where(low, below, above)

    for way, dy, dx, src, dst, copy in copies():

        @pl.when(inside(dy, dx))
        def _():
            copy.wait_send()


def halos(mesh_sizes, tracers, stream):
    n_fy, n_fx = mesh_sizes
    levels = stream.shape[0]
    groups = levels // GROUP
    parts = levels // (2 * GROUP)
    bf16 = jnp.bfloat16
    return pl.pallas_call(
        functools.partial(halo_kernel, n_fy, n_fx),
        out_shape=(
            jax.ShapeDtypeStruct((5, levels, 8, 128), jnp.float32),
            jax.ShapeDtypeStruct((2, groups, 72, 128), jnp.float32),
        ),
        in_specs=[pl.BlockSpec(memory_space=pl.ANY)] * 2,
        out_specs=(pl.BlockSpec(memory_space=pltpu.VMEM),) * 2,
        scratch_shapes=[
            pltpu.VMEM((5, levels, 64, 128), jnp.float32),
            pltpu.VMEM((2, 5, levels // 4, 16, 128), bf16),
            pltpu.VMEM((2, 5, levels // 4, 16, 128), bf16),
            pltpu.VMEM((2, groups, 64, 128), bf16),
            pltpu.VMEM((2, groups, 64, 128), bf16),
            pltpu.VMEM((2, groups, 16, 128), bf16),
            pltpu.VMEM((4, groups, 16, 128), bf16),
            pltpu.SemaphoreType.DMA((2, parts)),
            pltpu.SemaphoreType.DMA((8,)),
            pltpu.SemaphoreType.DMA((8,)),
        ],
        compiler_params=pltpu.CompilerParams(
            collective_id=0, has_side_effects=True, vmem_limit_bytes=40 << 20
        ),
        name="halo_exchange",
    )(tracers, stream)


def roll(cells, shift, axis):
    return pltpu.roll(cells, shift % cells.shape[axis], axis) if shift else cells


def stencil(stream, keep, hop):
    left = roll(stream, 1, 1)
    both = stream + left
    corner = (both + roll(both, 1, 0)) * 0.25
    west = corner - roll(corner, -1, 0)
    north = roll(corner, -1, 1) - corner
    east = roll(west, -1, 1)
    south = roll(north, -1, 0)
    centre = (
        1.0
        - jnp.maximum(east, 0.0)
        + jnp.minimum(west, 0.0)
        - jnp.maximum(south, 0.0)
        + jnp.minimum(north, 0.0)
    )
    return tuple(
        jnp.where(keep, w, 0.0)
        for w in (
            centre,
            jnp.maximum(west, 0.0),
            -jnp.minimum(east, 0.0),
            jnp.maximum(north, 0.0),
            -jnp.minimum(south, 0.0),
        )
    )


def advance(cells, weights):
    centre, west, east, north, south = weights
    for _ in range(SUBSTEPS):
        cells = (
            centre * cells
            + (west * roll(cells, 1, 1) + east * roll(cells, -1, 1))
            + (north * roll(cells, 1, 0) + south * roll(cells, -1, 0))
        )
    return cells


def column_kernel(
    n_fy,
    n_fx,
    offs,
    tr_hbm,
    st_hbm,
    row_halo,
    col_halo,
    land,
    pos,
    label,
    w_in_hbm,
    w_hid_hbm,
    w_out_hbm,
    bias,
    out_hbm,
    loss,
    state,
    stream,
    feats,
    w_in,
    w_hid,
    w_out,
    load_sem,
    weight_sem,
    out_sem,
):
    y = lax.axis_index("fy")
    x = lax.axis_index("fx")
    levels = st_hbm.shape[0]
    parts = 10
    per = levels // parts
    nf = 4 * levels

    def loads(part):
        span = pl.ds(part * per, per)
        return (
            pltpu.make_async_copy(tr_hbm.at[:, span], state.at[:, span], load_sem.at[0, part]),
            pltpu.make_async_copy(st_hbm.at[span], stream.at[span], load_sem.at[1, part]),
        )

    weights = [
        pltpu.make_async_copy(src, dst, weight_sem.at[i])
        for i, (src, dst) in enumerate(((w_in_hbm, w_in), (w_hid_hbm, w_hid), (w_out_hbm, w_out)))
    ]
    for part in range(parts):
        for copy in loads(part):
            copy.start()
    for copy in weights:
        copy.start()

    row = lax.broadcasted_iota(jnp.int32, (72, 128), 0)
    lane = lax.broadcasted_iota(jnp.int32, (72, 128), 1)
    row_ok = (
        (row < 64)
        | ((row < 68) & (y < n_fy - 1))
        | ((row >= 68) & (y > 0))
    )
    k = lane % 32
    strip_ok = row_ok & ((k >= 8) & (k < 24) | (k < 8) & (x > 0) | (k >= 24) & (x < n_fx - 1))

    def strip_of(main, west, east, f, at):
        here = jnp.where(k < 16, roll(main, at + 8, 1), roll(main, at + 16 - 120, 1))
        here = jnp.where(k < 8, roll(west, at + 4 - 4 * f, 1), here)
        return jnp.where(k >= 24, roll(east, at + 24 - 4 * f, 1), here)

    @pl.loop(0, levels)
    def _(level):
        @pl.when(level % per == 0)
        def _():
            for copy in loads(level // per):
                copy.wait()

        shift = (128 - (level % GROUP) * STEP) % 128
        west = pltpu.roll(col_halo[0, level // GROUP], shift, 1)
        east = pltpu.roll(col_halo[1, level // GROUP], shift, 1)

        psi = jnp.concatenate([stream[level], row_halo[4, level]], axis=0)
        one = jnp.where(lane < 32, strip_of(psi, west, east, 4, 0), 0.0)
        two = one + roll(one, 32, 1)
        psi_strip = two + roll(two, 64, 1)
        strip_weights = stencil(psi_strip, strip_ok, 1)

        cells = [
            jnp.concatenate([state[f, level], row_halo[f, level]], axis=0) for f in range(4)
        ]
        strip = strip_of(cells[0], west, east, 0, 0)
        for f in range(1, 4):
            mine = lane // 32 == f
            strip = jnp.where(mine, strip_of(cells[f], west, east, f, 32 * f), strip)
        strip = advance(strip, strip_weights)[0:64]

        main_weights = stencil(psi, row_ok, 1)
        for f in range(4):
            done = advance(cells[f], main_weights)[0:64]
            done = jnp.where(lane[0:64] < 4, roll(strip, -(32 * f + 8), 1), done)
            done = jnp.where(lane[0:64] >= 124, roll(strip, 104 - 32 * f, 1), done)
            state[f, level] = done

    for copy in weights:
        copy.wait()

    flat = state.reshape(nf * 64, 128)
    slot = lax.broadcasted_iota(jnp.int32, (WINDOW, CHUNK), 0)

    def window(i):
        return pl.multiple_of((offs[i] // 128) * 128, 128)

    def placing(i):
        return jnp.where(slot == pos[pl.ds(i, 1), :] - window(i), 1.0, 0.0).astype(jnp.bfloat16)

    feats[:, 0:128] = jnp.zeros((256, 128), jnp.bfloat16)
    tail_row = lax.broadcasted_iota(jnp.int32, (256 - nf, CHUNK), 0)

    @pl.loop(0, 32)
    def _(i):
        picked = jnp.concatenate(
            [
                flat[pl.ds(2 * i, nf, stride=64), :],
                flat[pl.ds(2 * i + 1, nf, stride=64), :],
            ],
            axis=1,
        )
        on_land = 4.0 * land[pl.ds(i, 1), :].astype(jnp.float32)
        tail = jnp.where(tail_row == 0, on_land, 0.0)
        chunk = jnp.concatenate([picked, tail], axis=0).astype(jnp.bfloat16)
        moved = lax.dot_general(
            chunk, placing(i), (((1,), (1,)), ((), ())), preferred_element_type=jnp.float32
        ).astype(jnp.bfloat16)
        at = window(i)
        feats[:, pl.ds(at, 128)] = feats[:, pl.ds(at, 128)] + moved[:, 0:128]
        feats[:, pl.ds(at + 128, 256)] = moved[:, 128:]

    def layer(w, inputs, b):
        summed = jnp.dot(w, inputs, preferred_element_type=jnp.float32) + b
        return jnp.maximum(summed, 0.15 * summed).astype(jnp.bfloat16)

    @pl.loop(0, (offs[32] + TILE - 1) // TILE)
    def _(t):
        cols = pl.ds(pl.multiple_of(t * TILE, TILE), TILE)
        hidden = layer(w_in[...], feats[:, cols], bias[:, 0:1])
        for l in range(w_hid.shape[0]):
            hidden = layer(w_hid[l], hidden, bias[:, l + 1 : l + 2])
        feats[:, cols] = (
            jnp.dot(w_out[...], hidden, preferred_element_type=jnp.float32) + bias[0:256, 7:8]
        ).astype(jnp.bfloat16)

    def out_copy(j):
        rows = pl.ds(pl.multiple_of(j * 8, 8), 8)
        return pltpu.make_async_copy(
            state.at[:, :, rows], out_hbm.at[:, :, rows], out_sem.at[j]
        )

    regime = lax.broadcasted_iota(jnp.int32, (8, CHUNK), 0)

    @pl.loop(0, 8)
    def _(j):
        for c in range(4):
            i = j * 4 + c
            back = jnp.dot(
                feats[:, pl.ds(window(i), WINDOW)],
                placing(i),
                preferred_element_type=jnp.float32,
            )
            for half in range(2):
                rows = pl.ds(2 * i + half, nf, stride=64)
                flat[rows, :] = flat[rows, :] + back[0:nf, half * 128 : half * 128 + 128]
            evidence = back[nf : nf + 8]
            alpha = 1.0 + (
                jnp.maximum(evidence, 0.0) + jnp.log1p(jnp.exp(-jnp.abs(evidence)))
            )
            alpha = jnp.where(regime < 4, alpha, 0.0)
            strength = jnp.sum(alpha, axis=0, keepdims=True)
            chosen = jnp.sum(
                jnp.where(regime == label[pl.ds(i, 1), :], alpha, 0.0), axis=0, keepdims=True
            )
            value = jnp.log(strength) - jnp.log(chosen)
            loss[pl.ds(i, 1), :] = jnp.where(pos[pl.ds(i, 1), :] >= 0, value, 0.0)
        out_copy(j).start()

    @pl.loop(0, 8)
    def _(j):
        out_copy(j).wait()


def columns(mesh_sizes, offs, *operands):
    n_fy, n_fx = mesh_sizes
    tracers, stream = operands[0], operands[1]
    levels = stream.shape[0]
    any_space = pl.BlockSpec(memory_space=pl.ANY)
    vmem = pl.BlockSpec(memory_space=pltpu.VMEM)
    return pl.pallas_call(
        functools.partial(column_kernel, n_fy, n_fx),
        out_shape=(
            jax.ShapeDtypeStruct(tracers.shape, jnp.float32),
            jax.ShapeDtypeStruct((32, CHUNK), jnp.float32),
        ),
        in_specs=[pl.BlockSpec(memory_space=pltpu.SMEM)]
        + [any_space] * 2
        + [vmem] * 5
        + [any_space] * 3
        + [vmem],
        out_specs=(any_space, vmem),
        scratch_shapes=[
            pltpu.VMEM(tracers.shape, jnp.float32),
            pltpu.VMEM(stream.shape, jnp.float32),
            pltpu.VMEM((256, MOST + 512), jnp.bfloat16),
            pltpu.VMEM((512, 256), jnp.bfloat16),
            pltpu.VMEM((6, 512, 512), jnp.bfloat16),
            pltpu.VMEM((256, 512), jnp.bfloat16),
            pltpu.SemaphoreType.DMA((2, 10)),
            pltpu.SemaphoreType.DMA((3,)),
            pltpu.SemaphoreType.DMA((8,)),
        ],
        compiler_params=pltpu.CompilerParams(vmem_limit_bytes=56 << 20),
        name="transport_and_network",
    )(offs, *operands)


def body(sizes, tracers, stream, land, convect, label, w_in, w_hid, b_hid, w_out, b_out):
    rows, cols = land.shape
    shape = (rows * cols // CHUNK, CHUNK)
    active = convect.reshape(shape)
    f32 = jnp.float32
    ones = active.astype(f32)
    tri = (jnp.arange(CHUNK)[:, None] <= jnp.arange(CHUNK)[None, :]).astype(f32)
    upto = jnp.dot(ones, tri, precision=lax.Precision.HIGHEST)
    before = (jnp.arange(shape[0] + 1)[:, None] > jnp.arange(shape[0])[None, :]).astype(f32)
    offs = jnp.sum(before * jnp.sum(ones, axis=1)[None, :], axis=1)
    pos = jnp.where(active > 0, (offs[:-1, None] + upto).astype(jnp.int32) - 1, -1)
    w_in = jnp.pad(w_in, ((0, 0), (0, 256 - w_in.shape[1])))
    bias = jnp.concatenate([b_hid, jnp.pad(b_out, (0, 512 - b_out.shape[0]))[None]], axis=0)
    bias = jnp.pad(bias.T, ((0, 0), (0, 120)))
    w_out = jnp.pad(w_out, ((0, 256 - w_out.shape[0]), (0, 0)))

    row_halo, col_halo = halos(sizes, tracers, stream)
    state, loss = columns(
        sizes,
        offs.astype(jnp.int32),
        tracers,
        stream,
        row_halo,
        col_halo,
        land.reshape(shape),
        pos,
        label.reshape(shape),
        w_in,
        w_hid,
        w_out,
        bias,
    )
    return (state, loss.reshape(rows, cols))


def solution(mesh):
    placed = (
        P(None, None, "fy", "fx"),
        P(None, "fy", "fx"),
        P("fy", "fx"),
        P("fy", "fx"),
        P("fy", "fx"),
        P(),
        P(),
        P(),
        P(),
        P(),
    )
    sizes = (mesh.shape["fy"], mesh.shape["fx"])
    return jax.shard_map(
        functools.partial(body, sizes),
        mesh=mesh,
        in_specs=placed,
        out_specs=(P(None, None, "fy", "fx"), P("fy", "fx")),
        check_vma=False,
    )
```

```python
import functools

import jax
import jax.numpy as jnp
from jax import lax
from jax.experimental import pallas as pl
from jax.experimental.pallas import tpu as pltpu
from jax.sharding import PartitionSpec as P

SUBSTEPS = 4
MESH = pl.DeviceIdType.MESH
CHUNK = 256
WINDOW = 384
TILE = 1024
MOST = 4096
GROUP = 6
STEP = 20

WAYS = ((-1, 0), (1, 0), (0, 1), (0, -1), (-1, 1), (1, 1), (-1, -1), (1, -1))


def halo_kernel(
    n_fy,
    n_fx,
    tr_hbm,
    st_hbm,
    row_out,
    col_out,
    fields,
    row_send,
    row_recv,
    col_send,
    col_recv,
    corner_send,
    corner_recv,
    load_sem,
    send_sem,
    recv_sem,
):
    y = lax.axis_index("fy")
    x = lax.axis_index("fx")
    levels = st_hbm.shape[0]
    per = 2 * GROUP
    parts = levels // per

    def inside(dy, dx):
        ok_y = (y + dy >= 0) & (y + dy < n_fy)
        ok_x = (x + dx >= 0) & (x + dx < n_fx)
        return ok_y & ok_x

    barrier = pltpu.get_barrier_semaphore()
    for dy, dx in WAYS:

        @pl.when(inside(dy, dx))
        def _():
            pl.semaphore_signal(barrier, inc=1, device_id=(x + dx, y + dy), device_id_type=MESH)

    def loads(part):
        span = pl.ds(part * per, per)
        return (
            pltpu.make_async_copy(
                tr_hbm.at[:, span], fields.at[pl.ds(0, 4), span], load_sem.at[0, part]
            ),
            pltpu.make_async_copy(st_hbm.at[span], fields.at[4, span], load_sem.at[1, part]),
        )

    for part in range(parts):
        for copy in loads(part):
            copy.start()

    lane = lax.broadcasted_iota(jnp.int32, (64, 128), 1)
    low = lax.broadcasted_iota(jnp.int32, (8, 128), 0) < 4

    @pl.loop(0, parts)
    def _(part):
        for copy in loads(part):
            copy.wait()
        first = part * per
        for half in range(2):
            east = jnp.zeros((64, 128), jnp.float32)
            west = jnp.zeros((64, 128), jnp.float32)
            for k in range(GROUP):
                for f in range(5):
                    cells = fields[f, first + half * GROUP + k]
                    at = k * STEP + f * 4
                    mask = (lane >= at) & (lane < at + 4)
                    east = jnp.where(mask, pltpu.roll(cells, (at - 124) % 128, 1), east)
                    west = jnp.where(mask, pltpu.roll(cells, at, 1) if at else cells, west)
            for d, packed in enumerate((east, west)):
                col_send[d, part * 2 + half] = packed.astype(jnp.bfloat16)
                ends = jnp.where(low, packed[0:8], packed[56:64])
                corner_send[d, part * 2 + half] = jnp.concatenate(
                    [ends, jnp.zeros_like(ends)], axis=0
                ).astype(jnp.bfloat16)
        for quad in range(per // 4):
            for f in range(5):
                heads = [fields[f, first + quad * 4 + j, 0:8] for j in range(4)]
                tails = [fields[f, first + quad * 4 + j, 56:64] for j in range(4)]
                up = [
                    jnp.where(low, heads[j], pltpu.roll(heads[j + 1], 4, 0)) for j in (0, 2)
                ]
                down = [
                    jnp.where(low, pltpu.roll(tails[j], 4, 0), tails[j + 1]) for j in (0, 2)
                ]
                row_send[0, f, part * 3 + quad] = jnp.concatenate(up, 0).astype(jnp.bfloat16)
                row_send[1, f, part * 3 + quad] = jnp.concatenate(down, 0).astype(jnp.bfloat16)

    tall = 1 + (y > 0).astype(jnp.int32) + (y < n_fy - 1).astype(jnp.int32)
    wide = 1 + (x > 0).astype(jnp.int32) + (x < n_fx - 1).astype(jnp.int32)
    pl.semaphore_wait(barrier, tall * wide - 1)

    def copies():
        for way, (dy, dx) in enumerate(WAYS):
            if way < 2:
                src, dst = row_send.at[way], row_recv.at[way]
            elif way < 4:
                src, dst = col_send.at[way - 2], col_recv.at[way - 2]
            else:
                src, dst = corner_send.at[(way - 4) // 2], corner_recv.at[way - 4]
            yield way, dy, dx, src, dst, pltpu.make_async_remote_copy(
                src_ref=src,
                dst_ref=dst,
                send_sem=send_sem.at[way],
                recv_sem=recv_sem.at[way],
                device_id=(x + dx, y + dy),
                device_id_type=MESH,
            )

    for way, dy, dx, src, dst, copy in copies():

        @pl.when(inside(dy, dx))
        def _():
            copy.start()

    for way, dy, dx, src, dst, copy in copies():

        @pl.when(inside(-dy, -dx))
        def _():
            copy.wait_recv()

        @pl.when(jnp.logical_not(inside(-dy, -dx)))
        def _():
            dst[...] = jnp.zeros(dst.shape, dst.dtype)

    @pl.loop(0, levels // 4)
    def _(quad):
        for f in range(5):
            below = row_recv[0, f, quad].astype(jnp.float32)
            above = row_recv[1, f, quad].astype(jnp.float32)
            for j in range(4):
                b = below[8 * (j // 2) : 8 * (j // 2) + 8]
                a = above[8 * (j // 2) : 8 * (j // 2) + 8]
                if j % 2:
                    b = pltpu.roll(b, 4, 0)
                else:
                    a = pltpu.roll(a, 4, 0)
                row_out[f, quad * 4 + j] = jnp.where(low, b, a)

    @pl.loop(0, levels // GROUP)
    def _(group):
        for d in range(2):
            col_out[d, group, 0:64] = col_recv[d, group].astype(jnp.float32)
            below = corner_recv[2 * d, group].astype(jnp.float32)[0:8]
            above = corner_recv[2 * d + 1, group].astype(jnp.float32)[0:8]
            col_out[d, group, 64:72] = jnp.where(low, below, above)

    for way, dy, dx, src, dst, copy in copies():

        @pl.when(inside(dy, dx))
        def _():
            copy.wait_send()


def halos(mesh_sizes, tracers, stream):
    n_fy, n_fx = mesh_sizes
    levels = stream.shape[0]
    groups = levels // GROUP
    parts = levels // (2 * GROUP)
    bf16 = jnp.bfloat16
    return pl.pallas_call(
        functools.partial(halo_kernel, n_fy, n_fx),
        out_shape=(
            jax.ShapeDtypeStruct((5, levels, 8, 128), jnp.float32),
            jax.ShapeDtypeStruct((2, groups, 72, 128), jnp.float32),
        ),
        in_specs=[pl.BlockSpec(memory_space=pl.ANY)] * 2,
        out_specs=(pl.BlockSpec(memory_space=pltpu.VMEM),) * 2,
        scratch_shapes=[
            pltpu.VMEM((5, levels, 64, 128), jnp.float32),
            pltpu.VMEM((2, 5, levels // 4, 16, 128), bf16),
            pltpu.VMEM((2, 5, levels // 4, 16, 128), bf16),
            pltpu.VMEM((2, groups, 64, 128), bf16),
            pltpu.VMEM((2, groups, 64, 128), bf16),
            pltpu.VMEM((2, groups, 16, 128), bf16),
            pltpu.VMEM((4, groups, 16, 128), bf16),
            pltpu.SemaphoreType.DMA((2, parts)),
            pltpu.SemaphoreType.DMA((8,)),
            pltpu.SemaphoreType.DMA((8,)),
        ],
        compiler_params=pltpu.CompilerParams(
            collective_id=0, has_side_effects=True, vmem_limit_bytes=60 << 20
        ),
        name="halo_exchange",
    )(tracers, stream)


SPAN = 249
GUARD = 96


def roll(cells, shift, axis):
    return pltpu.roll(cells, shift % cells.shape[axis], axis) if shift else cells


def around(cells, buffer, base):
    buffer[pl.ds(pl.multiple_of(base, 8), 88), :] = jnp.concatenate(
        [cells[64:72], cells, cells[0:8]], axis=0
    )
    return buffer[pl.ds(base + 7, 72), :], buffer[pl.ds(base + 9, 72), :]


def stencil(stream, keep, buffer, base):
    both = stream + roll(stream, 1, 1)
    before, after = around(both, buffer, base)
    corner = (both + before) * 0.25
    below = (after + both) * 0.25
    west = corner - below
    north = roll(corner, -1, 1) - corner
    south = roll(below, -1, 1) - below
    east = roll(west, -1, 1)
    centre = (
        1.0
        - jnp.maximum(east, 0.0)
        + jnp.minimum(west, 0.0)
        - jnp.maximum(south, 0.0)
        + jnp.minimum(north, 0.0)
    )
    return tuple(
        jnp.where(keep, w, 0.0)
        for w in (
            centre,
            jnp.maximum(west, 0.0),
            -jnp.minimum(east, 0.0),
            jnp.maximum(north, 0.0),
            -jnp.minimum(south, 0.0),
        )
    )


def advance(cells, weights, buffer, base):
    centre, west, east, north, south = weights
    before, after = around(cells, buffer, base)
    return (
        centre * cells
        + (west * roll(cells, 1, 1) + east * roll(cells, -1, 1))
        + (north * before + south * after)
    )


def column_kernel(
    n_fy,
    n_fx,
    tr_hbm,
    st_hbm,
    row_halo,
    col_halo,
    land,
    convect,
    label,
    w_in_raw,
    w_hid_hbm,
    w_out_raw,
    b_hid,
    b_out,
    out_hbm,
    loss,
    state,
    stream,
    by_row,
    back_rows,
    feats,
    w_in,
    w_hid,
    w_out,
    bias_rows,
    bias,
    place,
    pos,
    offs_v,
    offs,
    buf0,
    buf1,
    buf2,
    buf3,
    buf4,
    load_sem,
    weight_sem,
    out_sem,
):
    y = lax.axis_index("fy")
    x = lax.axis_index("fx")
    buffers = (buf0, buf1, buf2, buf3, buf4)
    levels = st_hbm.shape[0]
    parts = 10
    per = levels // parts
    nf = 4 * levels
    f32, bf16 = jnp.float32, jnp.bfloat16

    def loads(part):
        span = pl.ds(part * per, per)
        return (
            pltpu.make_async_copy(tr_hbm.at[:, span], state.at[:, span], load_sem.at[0, part]),
            pltpu.make_async_copy(st_hbm.at[span], stream.at[span], load_sem.at[1, part]),
        )

    for part in range(parts):
        for copy in loads(part):
            copy.start()
    hidden_copy = pltpu.make_async_copy(w_hid_hbm, w_hid, weight_sem.at[0])
    hidden_copy.start()

    w_in[...] = jnp.zeros(w_in.shape, bf16)
    w_in[:, 0 : w_in_raw.shape[1]] = w_in_raw[...]
    w_out[...] = jnp.zeros(w_out.shape, bf16)
    w_out[0 : w_out_raw.shape[0], :] = w_out_raw[...]
    bias_rows[...] = jnp.zeros(bias_rows.shape, f32)
    bias_rows[0:7, :] = b_hid[...]
    bias_rows[7:8, 0 : b_out.shape[1]] = b_out[...]
    bias[...] = bias_rows[...].T

    def iotas(shape):
        return [lax.broadcasted_iota(jnp.int32, shape, d) for d in (0, 1)]

    ones = convect[...].astype(f32)
    r, c = iotas((128, 128))
    upto = jnp.dot(ones, (r <= c).astype(f32), preferred_element_type=f32)
    totals = jnp.broadcast_to(jnp.sum(ones, axis=1, keepdims=True), (64, 128))
    r, c = iotas((72, 64))
    before = jnp.dot((r > c).astype(f32), totals, preferred_element_type=f32)
    pos[...] = jnp.where(convect[...] > 0, (before[0:64] + upto).astype(jnp.int32) - 1, -1)
    offs_v[...] = before.astype(jnp.int32)
    offs_copy = pltpu.make_async_copy(offs_v, offs, weight_sem.at[1])
    offs_copy.start()

    r, c = iotas((256, 256))
    side = r // 128
    for k in range(GROUP):
        j = r % 128 - k * STEP
        f, col = j // 4, j % 4
        good = (j >= 0) & (j < STEP)
        lane_at = 4 + 20 * side + col
        tracer = (f < 4) & (c == 32 * f + lane_at)
        psi = (f == 4) & (c >= 128) & (c % 32 == lane_at)
        place[k] = jnp.where(good & (tracer | psi), 1.0, 0.0).astype(bf16)

    row, lane = iotas((72, 128))
    row_ok = (
        (row < 64)
        | ((row < 68) & (y < n_fy - 1))
        | ((row >= 68) & (y > 0))
    )
    k32 = lane % 32
    middle = (k32 >= 8) & (k32 < 24)
    strip_ok = row_ok & (middle | (k32 < 8) & (x > 0) | (k32 >= 24) & (x < n_fx - 1))

    def local(main, at):
        return jnp.where(k32 < 16, roll(main, at + 8, 1), roll(main, at + 16 - 120, 1))

    @pl.loop(0, levels)
    def _(level):
        @pl.when(level % per == 0)
        def _():
            for copy in loads(level // per):
                copy.wait()

        base = (level % 2) * GUARD
        group = level // GROUP
        packed = jnp.concatenate([col_halo[0, group], col_halo[1, group]], axis=1).astype(bf16)
        beside = jnp.dot(packed, place[level % GROUP], preferred_element_type=f32)

        psi = jnp.concatenate([stream[level], row_halo[4, level]], axis=0)
        one = jnp.where(lane < 32, local(psi, 0), 0.0)
        two = one + roll(one, 32, 1)
        psi_strip = jnp.where(middle, two + roll(two, 64, 1), beside[:, 128:])
        strip_weights = stencil(psi_strip, strip_ok, buf4, base)
        main_weights = stencil(psi, row_ok, buf0, base)

        cells = [
            jnp.concatenate([state[f, level], row_halo[f, level]], axis=0) for f in range(4)
        ]
        strip = local(cells[0], 0)
        for f in range(1, 4):
            strip = jnp.where(lane // 32 == f, local(cells[f], 32 * f), strip)
        strip = jnp.where(middle, strip, beside[:, 0:128])

        for _ in range(SUBSTEPS):
            strip = advance(strip, strip_weights, buf4, base)
            for f in range(4):
                cells[f] = advance(cells[f], main_weights, buffers[f], base)

        strip = strip[0:64]
        for f in range(4):
            done = cells[f][0:64]
            done = jnp.where(lane[0:64] < 4, roll(strip, -(32 * f + 8), 1), done)
            done = jnp.where(lane[0:64] >= 124, roll(strip, 104 - 32 * f, 1), done)
            state[f, level] = done
            by_row[pl.ds(f * levels + level, 64, stride=SPAN), :] = done

    offs_copy.wait()
    hidden_copy.wait()

    slot, _ = iotas((WINDOW, CHUNK))

    def window(i):
        return pl.multiple_of((offs[2 * i, 0] // 128) * 128, 128)

    def pair(ref, i):
        return jnp.concatenate([ref[pl.ds(2 * i, 1), :], ref[pl.ds(2 * i + 1, 1), :]], axis=1)

    def placing(i):
        return jnp.where(slot == pair(pos, i) - window(i), 1.0, 0.0).astype(bf16)

    feats[:, 0:128] = jnp.zeros((256, 128), bf16)
    tail_row, _ = iotas((256 - nf, CHUNK))

    @pl.loop(0, 8)
    def _(j):
        moved = []
        for c in range(4):
            i = j * 4 + c
            picked = jnp.concatenate(
                [by_row[pl.ds((2 * i + half) * SPAN, nf), :] for half in range(2)], axis=1
            )
            on_land = 4.0 * pair(land, i).astype(f32)
            tail = jnp.where(tail_row == 0, on_land, 0.0)
            chunk = jnp.concatenate([picked, tail], axis=0).astype(bf16)
            moved.append(
                lax.dot_general(
                    chunk, placing(i), (((1,), (1,)), ((), ())), preferred_element_type=f32
                ).astype(bf16)
            )
        for c in range(4):
            at = window(j * 4 + c)
            feats[:, pl.ds(at, 128)] = feats[:, pl.ds(at, 128)] + moved[c][:, 0:128]
            feats[:, pl.ds(at + 128, 256)] = moved[c][:, 128:]

    def layer(w, inputs, b):
        summed = jnp.dot(w, inputs, preferred_element_type=f32) + b
        return jnp.maximum(summed, 0.15 * summed).astype(bf16)

    @pl.loop(0, (offs[64, 0] + TILE - 1) // TILE)
    def _(t):
        cols = pl.ds(pl.multiple_of(t * TILE, TILE), TILE)
        hidden = layer(w_in[...], feats[:, cols], bias[:, 0:1])
        for l in range(w_hid.shape[0]):
            hidden = layer(w_hid[l], hidden, bias[:, l + 1 : l + 2])
        feats[:, cols] = (
            jnp.dot(w_out[...], hidden, preferred_element_type=f32) + bias[0:256, 7:8]
        ).astype(bf16)

    def out_copy(j):
        rows = pl.ds(pl.multiple_of(j * 8, 8), 8)
        return pltpu.make_async_copy(
            state.at[:, :, rows], out_hbm.at[:, :, rows], out_sem.at[j]
        )

    regime, _ = iotas((8, 8 * 128))

    @pl.loop(0, 8)
    def _(j):
        start = (j % 2) * (8 * SPAN)
        evidence = []
        for c in range(4):
            i = j * 4 + c
            back = jnp.dot(
                feats[:, pl.ds(window(i), WINDOW)], placing(i), preferred_element_type=f32
            )
            for half in range(2):
                back_rows[pl.ds(start + (2 * c + half) * SPAN, nf), :] = back[
                    0:nf, half * 128 : half * 128 + 128
                ]
            evidence.append(back[nf : nf + 8])
        rows = pl.ds(pl.multiple_of(j * 8, 8), 8)
        for f in range(4):
            for level in range(levels):
                state[f, level, rows] = (
                    state[f, level, rows]
                    + back_rows[pl.ds(start + f * levels + level, 8, stride=SPAN), :]
                )
        out_copy(j).start()
        evidence = jnp.concatenate(evidence, axis=1)
        alpha = 1.0 + (jnp.maximum(evidence, 0.0) + jnp.log1p(jnp.exp(-jnp.abs(evidence))))
        alpha = jnp.where(regime < 4, alpha, 0.0)
        strength = jnp.sum(alpha, axis=0, keepdims=True)
        labels = jnp.concatenate([label[pl.ds(j * 8 + q, 1), :] for q in range(8)], axis=1)
        chosen = jnp.sum(jnp.where(regime == labels, alpha, 0.0), axis=0, keepdims=True)
        value = jnp.log(strength) - jnp.log(chosen)
        for q in range(8):
            at = pl.ds(j * 8 + q, 1)
            loss[at, :] = jnp.where(
                convect[at, :] > 0, value[:, q * 128 : q * 128 + 128], 0.0
            )

    @pl.loop(0, 8)
    def _(j):
        out_copy(j).wait()


def columns(mesh_sizes, *operands):
    n_fy, n_fx = mesh_sizes
    tracers, stream = operands[0], operands[1]
    any_space = pl.BlockSpec(memory_space=pl.ANY)
    vmem = pl.BlockSpec(memory_space=pltpu.VMEM)
    f32, bf16 = jnp.float32, jnp.bfloat16
    return pl.pallas_call(
        functools.partial(column_kernel, n_fy, n_fx),
        out_shape=(
            jax.ShapeDtypeStruct(tracers.shape, f32),
            jax.ShapeDtypeStruct((64, 128), f32),
        ),
        in_specs=[any_space] * 2 + [vmem] * 6 + [any_space] + [vmem] * 3,
        out_specs=(any_space, vmem),
        scratch_shapes=[
            pltpu.VMEM(tracers.shape, f32),
            pltpu.VMEM(stream.shape, f32),
            pltpu.VMEM((64 * SPAN, 128), f32),
            pltpu.VMEM((16 * SPAN, 128), f32),
            pltpu.VMEM((256, MOST + 512), bf16),
            pltpu.VMEM((512, 256), bf16),
            pltpu.VMEM((6, 512, 512), bf16),
            pltpu.VMEM((256, 512), bf16),
            pltpu.VMEM((128, 512), f32),
            pltpu.VMEM((512, 128), f32),
            pltpu.VMEM((GROUP, 256, 256), bf16),
            pltpu.VMEM((64, 128), jnp.int32),
            pltpu.VMEM((72, 128), jnp.int32),
            pltpu.SMEM((72, 128), jnp.int32),
        ]
        + [pltpu.VMEM((2 * GUARD, 128), f32)] * 5
        + [
            pltpu.SemaphoreType.DMA((2, 10)),
            pltpu.SemaphoreType.DMA((2,)),
            pltpu.SemaphoreType.DMA((8,)),
        ],
        compiler_params=pltpu.CompilerParams(vmem_limit_bytes=60 << 20),
        name="transport_and_network",
    )(*operands)


def body(sizes, tracers, stream, land, convect, label, w_in, w_hid, b_hid, w_out, b_out):
    row_halo, col_halo = halos(sizes, tracers, stream)
    return columns(
        sizes,
        tracers,
        stream,
        row_halo,
        col_halo,
        land,
        convect,
        label,
        w_in,
        w_hid,
        w_out,
        b_hid,
        b_out.reshape(1, -1),
    )


def solution(mesh):
    placed = (
        P(None, None, "fy", "fx"),
        P(None, "fy", "fx"),
        P("fy", "fx"),
        P("fy", "fx"),
        P("fy", "fx"),
        P(),
        P(),
        P(),
        P(),
        P(),
    )
    sizes = (mesh.shape["fy"], mesh.shape["fx"])
    return jax.shard_map(
        functools.partial(body, sizes),
        mesh=mesh,
        in_specs=placed,
        out_specs=(P(None, None, "fy", "fx"), P("fy", "fx")),
        check_vma=False,
    )
```

```python
import functools

import jax
import jax.numpy as jnp
from jax import lax
from jax.experimental import pallas as pl
from jax.experimental.pallas import tpu as pltpu
from jax.sharding import PartitionSpec as P

SUBSTEPS = 4
MESH = pl.DeviceIdType.MESH
CHUNK = 128
WINDOW = 256
TILE = 1024
MOST = 4096
GROUP = 6
STEP = 20

WAYS = ((-1, 0), (1, 0), (0, 1), (0, -1), (-1, 1), (1, 1), (-1, -1), (1, -1))


def halo_kernel(
    n_fy,
    n_fx,
    tr_hbm,
    st_hbm,
    row_out,
    col_out,
    fields,
    row_send,
    row_recv,
    col_send,
    col_recv,
    corner_send,
    corner_recv,
    load_sem,
    send_sem,
    recv_sem,
):
    y = lax.axis_index("fy")
    x = lax.axis_index("fx")
    levels = st_hbm.shape[0]
    per = 2 * GROUP
    parts = levels // per

    def inside(dy, dx):
        ok_y = (y + dy >= 0) & (y + dy < n_fy)
        ok_x = (x + dx >= 0) & (x + dx < n_fx)
        return ok_y & ok_x

    barrier = pltpu.get_barrier_semaphore()
    for dy, dx in WAYS:

        @pl.when(inside(dy, dx))
        def _():
            pl.semaphore_signal(barrier, inc=1, device_id=(x + dx, y + dy), device_id_type=MESH)

    def loads(part):
        span = pl.ds(part * per, per)
        return (
            pltpu.make_async_copy(
                tr_hbm.at[:, span], fields.at[pl.ds(0, 4), span], load_sem.at[0, part]
            ),
            pltpu.make_async_copy(st_hbm.at[span], fields.at[4, span], load_sem.at[1, part]),
        )

    for part in range(parts):
        for copy in loads(part):
            copy.start()

    lane = lax.broadcasted_iota(jnp.int32, (64, 128), 1)
    low = lax.broadcasted_iota(jnp.int32, (8, 128), 0) < 4

    def copies(ways):
        for way in ways:
            dy, dx = WAYS[way]
            if way < 2:
                src, dst = row_send.at[way], row_recv.at[way]
            elif way < 4:
                src, dst = col_send.at[way - 2], col_recv.at[way - 2]
            else:
                src, dst = corner_send.at[(way - 4) // 2], corner_recv.at[way - 4]
            yield dy, dx, dst, pltpu.make_async_remote_copy(
                src_ref=src,
                dst_ref=dst,
                send_sem=send_sem.at[way],
                recv_sem=recv_sem.at[way],
                device_id=(x + dx, y + dy),
                device_id_type=MESH,
            )

    def start(ways):
        for dy, dx, _, copy in copies(ways):

            @pl.when(inside(dy, dx))
            def _():
                copy.start()

    def arrive(ways):
        for dy, dx, dst, copy in copies(ways):

            @pl.when(inside(-dy, -dx))
            def _():
                copy.wait_recv()

            @pl.when(jnp.logical_not(inside(-dy, -dx)))
            def _():
                dst[...] = jnp.zeros(dst.shape, dst.dtype)

    @pl.loop(0, parts)
    def _(part):
        for copy in loads(part):
            copy.wait()
        first = part * per
        for quad in range(per // 4):
            for f in range(5):
                heads = [fields[f, first + quad * 4 + j, 0:8] for j in range(4)]
                tails = [fields[f, first + quad * 4 + j, 56:64] for j in range(4)]
                up = [
                    jnp.where(low, heads[j], pltpu.roll(heads[j + 1], 4, 0)) for j in (0, 2)
                ]
                down = [
                    jnp.where(low, pltpu.roll(tails[j], 4, 0), tails[j + 1]) for j in (0, 2)
                ]
                row_send[0, f, part * 3 + quad] = jnp.concatenate(up, 0).astype(jnp.bfloat16)
                row_send[1, f, part * 3 + quad] = jnp.concatenate(down, 0).astype(jnp.bfloat16)

    tall = 1 + (y > 0).astype(jnp.int32) + (y < n_fy - 1).astype(jnp.int32)
    wide = 1 + (x > 0).astype(jnp.int32) + (x < n_fx - 1).astype(jnp.int32)
    pl.semaphore_wait(barrier, tall * wide - 1)
    start((0, 1))

    @pl.loop(0, parts)
    def _(part):
        first = part * per
        for half in range(2):
            east = jnp.zeros((64, 128), jnp.float32)
            west = jnp.zeros((64, 128), jnp.float32)
            for k in range(GROUP):
                for f in range(5):
                    cells = fields[f, first + half * GROUP + k]
                    at = k * STEP + f * 4
                    mask = (lane >= at) & (lane < at + 4)
                    east = jnp.where(mask, pltpu.roll(cells, (at - 124) % 128, 1), east)
                    west = jnp.where(mask, pltpu.roll(cells, at, 1) if at else cells, west)
            for d, packed in enumerate((east, west)):
                col_send[d, part * 2 + half] = packed.astype(jnp.bfloat16)
                ends = jnp.where(low, packed[0:8], packed[56:64])
                corner_send[d, part * 2 + half] = jnp.concatenate(
                    [ends, jnp.zeros_like(ends)], axis=0
                ).astype(jnp.bfloat16)

    start(range(2, 8))
    arrive((0, 1))

    @pl.loop(0, levels // 4)
    def _(quad):
        for f in range(5):
            below = row_recv[0, f, quad].astype(jnp.float32)
            above = row_recv[1, f, quad].astype(jnp.float32)
            for j in range(4):
                b = below[8 * (j // 2) : 8 * (j // 2) + 8]
                a = above[8 * (j // 2) : 8 * (j // 2) + 8]
                if j % 2:
                    b = pltpu.roll(b, 4, 0)
                else:
                    a = pltpu.roll(a, 4, 0)
                row_out[f, quad * 4 + j] = jnp.where(low, b, a)

    arrive(range(2, 8))

    @pl.loop(0, levels // GROUP)
    def _(group):
        for d in range(2):
            col_out[d, group, 0:64] = col_recv[d, group].astype(jnp.float32)
            below = corner_recv[2 * d, group].astype(jnp.float32)[0:8]
            above = corner_recv[2 * d + 1, group].astype(jnp.float32)[0:8]
            col_out[d, group, 64:72] = jnp.where(low, below, above)

    for dy, dx, _, copy in copies(range(8)):

        @pl.when(inside(dy, dx))
        def _():
            copy.wait_send()


def halos(mesh_sizes, tracers, stream):
    n_fy, n_fx = mesh_sizes
    levels = stream.shape[0]
    groups = levels // GROUP
    parts = levels // (2 * GROUP)
    bf16 = jnp.bfloat16
    return pl.pallas_call(
        functools.partial(halo_kernel, n_fy, n_fx),
        out_shape=(
            jax.ShapeDtypeStruct((5, levels, 8, 128), jnp.float32),
            jax.ShapeDtypeStruct((2, groups, 72, 128), jnp.float32),
        ),
        in_specs=[pl.BlockSpec(memory_space=pl.ANY)] * 2,
        out_specs=(pl.BlockSpec(memory_space=pltpu.VMEM),) * 2,
        scratch_shapes=[
            pltpu.VMEM((5, levels, 64, 128), jnp.float32),
            pltpu.VMEM((2, 5, levels // 4, 16, 128), bf16),
            pltpu.VMEM((2, 5, levels // 4, 16, 128), bf16),
            pltpu.VMEM((2, groups, 64, 128), bf16),
            pltpu.VMEM((2, groups, 64, 128), bf16),
            pltpu.VMEM((2, groups, 16, 128), bf16),
            pltpu.VMEM((4, groups, 16, 128), bf16),
            pltpu.SemaphoreType.DMA((2, parts)),
            pltpu.SemaphoreType.DMA((8,)),
            pltpu.SemaphoreType.DMA((8,)),
        ],
        compiler_params=pltpu.CompilerParams(
            collective_id=0, has_side_effects=True, vmem_limit_bytes=60 << 20
        ),
        name="halo_exchange",
    )(tracers, stream)


SPAN = 249
GUARD = 96


def roll(cells, shift, axis):
    return pltpu.roll(cells, shift % cells.shape[axis], axis) if shift else cells


def keep_rows(tiles, buffer, base):
    for i, tile in enumerate([tiles[8], *tiles, tiles[0]]):
        buffer[pl.ds(pl.multiple_of(base + 8 * i, 8), 8), :] = tile


def around(cells, buffer, base):
    buffer[pl.ds(pl.multiple_of(base, 8), 88), :] = jnp.concatenate(
        [cells[64:72], cells, cells[0:8]], axis=0
    )
    return buffer[pl.ds(base + 7, 72), :], buffer[pl.ds(base + 9, 72), :]


def stencil(stream, keep, buffer, base):
    both = stream + roll(stream, 1, 1)
    before, after = around(both, buffer, base)
    corner = (both + before) * 0.25
    below = (after + both) * 0.25
    west = corner - below
    north = roll(corner, -1, 1) - corner
    south = roll(below, -1, 1) - below
    east = roll(west, -1, 1)
    centre = (
        1.0
        - jnp.maximum(east, 0.0)
        + jnp.minimum(west, 0.0)
        - jnp.maximum(south, 0.0)
        + jnp.minimum(north, 0.0)
    )
    return tuple(
        jnp.where(keep, w, 0.0)
        for w in (
            centre,
            jnp.maximum(west, 0.0),
            -jnp.minimum(east, 0.0),
            jnp.maximum(north, 0.0),
            -jnp.minimum(south, 0.0),
        )
    )


def advance(tile, weights, buffer, at):
    centre, west, east, north, south = weights
    return (
        centre * tile
        + (west * roll(tile, 1, 1) + east * roll(tile, -1, 1))
        + (north * buffer[pl.ds(at - 1, 8), :] + south * buffer[pl.ds(at + 1, 8), :])
    )


def tiles_of(cells):
    return [cells[8 * i : 8 * i + 8] for i in range(cells.shape[0] // 8)]


def column_kernel(
    n_fy,
    n_fx,
    tr_hbm,
    st_hbm,
    row_halo,
    col_halo,
    land,
    convect,
    label,
    w_in_raw,
    w_hid_hbm,
    w_out_raw,
    b_hid,
    b_out,
    out_hbm,
    loss,
    state,
    stream,
    by_row,
    back_rows,
    feats,
    w_in,
    w_hid,
    w_out,
    bias_rows,
    bias,
    place,
    placing,
    pos,
    offs_v,
    offs,
    *rest,
):
    y = lax.axis_index("fy")
    x = lax.axis_index("fx")
    buffers = (rest[0:5], rest[5:10])
    load_sem, weight_sem, out_sem = rest[10:]
    levels = st_hbm.shape[0]
    parts = 10
    per = levels // parts
    nf = 4 * levels
    f32, bf16 = jnp.float32, jnp.bfloat16

    def loads(part):
        span = pl.ds(part * per, per)
        return (
            pltpu.make_async_copy(tr_hbm.at[:, span], state.at[:, span], load_sem.at[0, part]),
            pltpu.make_async_copy(st_hbm.at[span], stream.at[span], load_sem.at[1, part]),
        )

    for part in range(parts):
        for copy in loads(part):
            copy.start()
    hidden_copy = pltpu.make_async_copy(w_hid_hbm, w_hid, weight_sem.at[0])
    hidden_copy.start()

    w_out[...] = jnp.zeros(w_out.shape, bf16)
    w_out[0 : w_in_raw.shape[0], :] = w_in_raw[...]
    w_in[...] = w_out[...].astype(f32).T.astype(bf16)
    w_out[240:256, :] = jnp.zeros((16, 512), bf16)
    w_out[0 : w_out_raw.shape[0], :] = w_out_raw[...]
    bias_rows[...] = jnp.zeros(bias_rows.shape, f32)
    bias_rows[0:7, :] = b_hid[...]
    bias_rows[7:8, 0 : b_out.shape[1]] = b_out[...]
    bias[...] = bias_rows[...].T

    def iotas(shape):
        return [lax.broadcasted_iota(jnp.int32, shape, d) for d in (0, 1)]

    ones = convect[...].astype(f32)
    r, c = iotas((128, 128))
    upto = jnp.dot(ones, (r <= c).astype(f32), preferred_element_type=f32)
    totals = jnp.broadcast_to(jnp.sum(ones, axis=1, keepdims=True), (64, 128))
    r, c = iotas((72, 64))
    before = jnp.dot((r > c).astype(f32), totals, preferred_element_type=f32)
    pos[...] = jnp.where(convect[...] > 0, (before[0:64] + upto).astype(jnp.int32) - 1, -1)
    offs_v[...] = before.astype(jnp.int32)
    offs_copy = pltpu.make_async_copy(offs_v, offs, weight_sem.at[1])
    offs_copy.start()

    r, c = iotas((256, 256))
    side = r // 128
    for k in range(GROUP):
        j = r % 128 - k * STEP
        f, col = j // 4, j % 4
        good = (j >= 0) & (j < STEP)
        lane_at = 4 + 20 * side + col
        tracer = (f < 4) & (c == 32 * f + lane_at)
        psi = (f == 4) & (c >= 128) & (c % 32 == lane_at)
        place[k] = jnp.where(good & (tracer | psi), 1.0, 0.0).astype(bf16)

    row, lane = iotas((72, 128))
    row_ok = (
        (row < 64)
        | ((row < 68) & (y < n_fy - 1))
        | ((row >= 68) & (y > 0))
    )
    k32 = lane % 32
    middle = (k32 >= 8) & (k32 < 24)
    strip_ok = row_ok & (middle | (k32 < 8) & (x > 0) | (k32 >= 24) & (x < n_fx - 1))

    def local(main, at):
        return jnp.where(k32 < 16, roll(main, at + 8, 1), roll(main, at + 16 - 120, 1))

    @pl.loop(0, levels)
    def _(level):
        @pl.when(level % per == 0)
        def _():
            for copy in loads(level // per):
                copy.wait()

        base = (level % 2) * GUARD
        group = level // GROUP
        packed = jnp.concatenate([col_halo[0, group], col_halo[1, group]], axis=1).astype(bf16)
        beside = jnp.dot(packed, place[level % GROUP], preferred_element_type=f32)

        psi = jnp.concatenate([stream[level], row_halo[4, level]], axis=0)
        one = jnp.where(lane < 32, local(psi, 0), 0.0)
        two = one + roll(one, 32, 1)
        psi_strip = jnp.where(middle, two + roll(two, 64, 1), beside[:, 128:])
        strip_weights = stencil(psi_strip, strip_ok, buffers[1][4], base)
        main_weights = stencil(psi, row_ok, buffers[1][0], base)

        cells = [
            jnp.concatenate([state[f, level], row_halo[f, level]], axis=0) for f in range(4)
        ]
        strip = local(cells[0], 0)
        for f in range(1, 4):
            strip = jnp.where(lane // 32 == f, local(cells[f], 32 * f), strip)
        strip = jnp.where(middle, strip, beside[:, 0:128])

        fields = [tiles_of(c) for c in cells] + [tiles_of(strip)]
        main_tiles = list(zip(*map(tiles_of, main_weights)))
        strip_tiles = list(zip(*map(tiles_of, strip_weights)))
        for substep in range(SUBSTEPS):
            held = buffers[substep % 2]
            for f in range(5):
                keep_rows(fields[f], held[f], base)
            count = 9 if substep < SUBSTEPS - 1 else 8
            for i in range(count):
                for f in range(5):
                    fields[f][i] = advance(
                        fields[f][i],
                        main_tiles[i] if f < 4 else strip_tiles[i],
                        held[f],
                        base + 8 + 8 * i,
                    )
        cells = [jnp.concatenate(tiles[0:8], axis=0) for tiles in fields]
        strip = cells[4]
        for f in range(4):
            done = cells[f]
            done = jnp.where(lane[0:64] < 4, roll(strip, -(32 * f + 8), 1), done)
            done = jnp.where(lane[0:64] >= 124, roll(strip, 104 - 32 * f, 1), done)
            state[f, level] = done
            by_row[pl.ds(f * levels + level, 64, stride=SPAN), :] = done

    offs_copy.wait()
    hidden_copy.wait()

    slot, _ = iotas((WINDOW, CHUNK))

    def window(i):
        return pl.multiple_of((offs[i, 0] // 128) * 128, 128)

    feats[:, 0:128] = jnp.zeros((256, 128), bf16)
    tail_row, _ = iotas((256 - nf, CHUNK))

    @pl.loop(0, 8)
    def _(j):
        moved = []
        for q in range(8):
            i = j * 8 + q
            picked = by_row[pl.ds(i * SPAN, nf), :]
            on_land = 4.0 * land[pl.ds(i, 1), :].astype(f32)
            tail = jnp.where(tail_row == 0, on_land, 0.0)
            chunk = jnp.concatenate([picked, tail], axis=0).astype(bf16)
            hot = jnp.where(slot == pos[pl.ds(i, 1), :] - window(i), 1.0, 0.0).astype(bf16)
            placing[i] = hot
            moved.append(
                lax.dot_general(
                    chunk, hot, (((1,), (1,)), ((), ())), preferred_element_type=f32
                ).astype(bf16)
            )
        for q in range(8):
            at = window(j * 8 + q)
            feats[:, pl.ds(at, 128)] = feats[:, pl.ds(at, 128)] + moved[q][:, 0:128]
            feats[:, pl.ds(at + 128, 128)] = moved[q][:, 128:]

    def layer(w, inputs, b):
        summed = jnp.dot(w, inputs, preferred_element_type=f32) + b
        return jnp.maximum(summed, 0.15 * summed).astype(bf16)

    @pl.loop(0, (offs[64, 0] + TILE - 1) // TILE)
    def _(t):
        cols = pl.ds(pl.multiple_of(t * TILE, TILE), TILE)
        hidden = layer(w_in[...], feats[:, cols], bias[:, 0:1])
        for l in range(w_hid.shape[0]):
            hidden = layer(w_hid[l], hidden, bias[:, l + 1 : l + 2])
        feats[:, cols] = (
            jnp.dot(w_out[...], hidden, preferred_element_type=f32) + bias[0:256, 7:8]
        ).astype(bf16)

    def out_copy(j):
        rows = pl.ds(pl.multiple_of(j * 8, 8), 8)
        return pltpu.make_async_copy(
            state.at[:, :, rows], out_hbm.at[:, :, rows], out_sem.at[j]
        )

    regime, _ = iotas((8, 8 * 128))

    @pl.loop(0, 8)
    def _(j):
        start = (j % 2) * (8 * SPAN)
        evidence = []
        for q in range(8):
            i = j * 8 + q
            back = jnp.dot(
                feats[:, pl.ds(window(i), WINDOW)], placing[i], preferred_element_type=f32
            )
            back_rows[pl.ds(start + q * SPAN, nf), :] = back[0:nf]
            evidence.append(back[nf : nf + 8])
        rows = pl.ds(pl.multiple_of(j * 8, 8), 8)
        for f in range(4):
            for level in range(levels):
                state[f, level, rows] = (
                    state[f, level, rows]
                    + back_rows[pl.ds(start + f * levels + level, 8, stride=SPAN), :]
                )
        out_copy(j).start()
        evidence = jnp.concatenate(evidence, axis=1)
        alpha = 1.0 + (jnp.maximum(evidence, 0.0) + jnp.log1p(jnp.exp(-jnp.abs(evidence))))
        alpha = jnp.where(regime < 4, alpha, 0.0)
        strength = jnp.sum(alpha, axis=0, keepdims=True)
        labels = jnp.concatenate([label[pl.ds(j * 8 + q, 1), :] for q in range(8)], axis=1)
        chosen = jnp.sum(jnp.where(regime == labels, alpha, 0.0), axis=0, keepdims=True)
        value = jnp.log(strength) - jnp.log(chosen)
        for q in range(8):
            at = pl.ds(j * 8 + q, 1)
            loss[at, :] = jnp.where(
                convect[at, :] > 0, value[:, q * 128 : q * 128 + 128], 0.0
            )

    @pl.loop(0, 8)
    def _(j):
        out_copy(j).wait()


def columns(mesh_sizes, *operands):
    n_fy, n_fx = mesh_sizes
    tracers, stream = operands[0], operands[1]
    any_space = pl.BlockSpec(memory_space=pl.ANY)
    vmem = pl.BlockSpec(memory_space=pltpu.VMEM)
    f32, bf16 = jnp.float32, jnp.bfloat16
    return pl.pallas_call(
        functools.partial(column_kernel, n_fy, n_fx),
        out_shape=(
            jax.ShapeDtypeStruct(tracers.shape, f32),
            jax.ShapeDtypeStruct((64, 128), f32),
        ),
        in_specs=[any_space] * 2 + [vmem] * 6 + [any_space] + [vmem] * 3,
        out_specs=(any_space, vmem),
        scratch_shapes=[
            pltpu.VMEM(tracers.shape, f32),
            pltpu.VMEM(stream.shape, f32),
            pltpu.VMEM((64 * SPAN, 128), f32),
            pltpu.VMEM((16 * SPAN, 128), f32),
            pltpu.VMEM((256, MOST + 512), bf16),
            pltpu.VMEM((512, 256), bf16),
            pltpu.VMEM((6, 512, 512), bf16),
            pltpu.VMEM((256, 512), bf16),
            pltpu.VMEM((128, 512), f32),
            pltpu.VMEM((512, 128), f32),
            pltpu.VMEM((GROUP, 256, 256), bf16),
            pltpu.VMEM((64, WINDOW, CHUNK), bf16),
            pltpu.VMEM((64, 128), jnp.int32),
            pltpu.VMEM((72, 128), jnp.int32),
            pltpu.SMEM((72, 128), jnp.int32),
        ]
        + [pltpu.VMEM((2 * GUARD, 128), f32)] * 10
        + [
            pltpu.SemaphoreType.DMA((2, 10)),
            pltpu.SemaphoreType.DMA((2,)),
            pltpu.SemaphoreType.DMA((8,)),
        ],
        compiler_params=pltpu.CompilerParams(vmem_limit_bytes=60 << 20),
        name="transport_and_network",
    )(*operands)


def body(sizes, tracers, stream, land, convect, label, w_in, w_hid, b_hid, w_out, b_out):
    row_halo, col_halo = halos(sizes, tracers, stream)
    return columns(
        sizes,
        tracers,
        stream,
        row_halo,
        col_halo,
        land,
        convect,
        label,
        w_in.T,
        w_hid,
        w_out,
        b_hid,
        b_out.reshape(1, -1),
    )


def solution(mesh):
    placed = (
        P(None, None, "fy", "fx"),
        P(None, "fy", "fx"),
        P("fy", "fx"),
        P("fy", "fx"),
        P("fy", "fx"),
        P(),
        P(),
        P(),
        P(),
        P(),
    )
    sizes = (mesh.shape["fy"], mesh.shape["fx"])
    return jax.shard_map(
        functools.partial(body, sizes),
        mesh=mesh,
        in_specs=placed,
        out_specs=(P(None, None, "fy", "fx"), P("fy", "fx")),
        check_vma=False,
    )
```

```python
import functools

import jax
import jax.numpy as jnp
from jax import lax
from jax.experimental import pallas as pl
from jax.experimental.pallas import tpu as pltpu
from jax.sharding import PartitionSpec as P

SUBSTEPS = 4
MESH = pl.DeviceIdType.MESH
CHUNK = 128
WINDOW = 256
TILE = 1024
MOST = 4096
GROUP = 6
STEP = 20

WAYS = ((-1, 0), (1, 0), (0, 1), (0, -1), (-1, 1), (1, 1), (-1, -1), (1, -1))


def halo_kernel(
    n_fy,
    n_fx,
    tr_hbm,
    st_hbm,
    row_out,
    col_out,
    fields,
    row_send,
    row_recv,
    col_send,
    col_recv,
    corner_send,
    corner_recv,
    pick,
    load_sem,
    send_sem,
    recv_sem,
):
    y = lax.axis_index("fy")
    x = lax.axis_index("fx")
    levels = st_hbm.shape[0]
    per = 2 * GROUP
    parts = levels // per

    def inside(dy, dx):
        ok_y = (y + dy >= 0) & (y + dy < n_fy)
        ok_x = (x + dx >= 0) & (x + dx < n_fx)
        return ok_y & ok_x

    barrier = pltpu.get_barrier_semaphore()
    for dy, dx in WAYS:

        @pl.when(inside(dy, dx))
        def _():
            pl.semaphore_signal(barrier, inc=1, device_id=(x + dx, y + dy), device_id_type=MESH)

    def loads(part):
        span = pl.ds(part * per, per)
        return (
            pltpu.make_async_copy(
                tr_hbm.at[:, span], fields.at[pl.ds(0, 4), span], load_sem.at[0, part]
            ),
            pltpu.make_async_copy(st_hbm.at[span], fields.at[4, span], load_sem.at[1, part]),
        )

    for part in range(parts):
        for copy in loads(part):
            copy.start()

    r = lax.broadcasted_iota(jnp.int32, (640, 256), 0)
    c = lax.broadcasted_iota(jnp.int32, (640, 256), 1)
    col = r % 128 - jnp.where(c < 128, 124, 0)
    at = jnp.where((col >= 0) & (col < 4), c % 128 - 4 * (r // 128) - col, -1)
    for k in range(GROUP):
        pick[k] = jnp.where(at == k * STEP, 1.0, 0.0).astype(jnp.bfloat16)

    low = lax.broadcasted_iota(jnp.int32, (8, 128), 0) < 4

    def copies(ways):
        for way in ways:
            dy, dx = WAYS[way]
            if way < 2:
                src, dst = row_send.at[way], row_recv.at[way]
            elif way < 4:
                src, dst = col_send.at[way - 2], col_recv.at[way - 2]
            else:
                src, dst = corner_send.at[(way - 4) // 2], corner_recv.at[way - 4]
            yield dy, dx, dst, pltpu.make_async_remote_copy(
                src_ref=src,
                dst_ref=dst,
                send_sem=send_sem.at[way],
                recv_sem=recv_sem.at[way],
                device_id=(x + dx, y + dy),
                device_id_type=MESH,
            )

    def start(ways):
        for dy, dx, _, copy in copies(ways):

            @pl.when(inside(dy, dx))
            def _():
                copy.start()

    def arrive(ways):
        for dy, dx, dst, copy in copies(ways):

            @pl.when(inside(-dy, -dx))
            def _():
                copy.wait_recv()

            @pl.when(jnp.logical_not(inside(-dy, -dx)))
            def _():
                dst[...] = jnp.zeros(dst.shape, dst.dtype)

    @pl.loop(0, parts)
    def _(part):
        for copy in loads(part):
            copy.wait()
        first = part * per
        for quad in range(per // 4):
            for f in range(5):
                heads = [fields[f, first + quad * 4 + j, 0:8] for j in range(4)]
                tails = [fields[f, first + quad * 4 + j, 56:64] for j in range(4)]
                up = [
                    jnp.where(low, heads[j], pltpu.roll(heads[j + 1], 4, 0)) for j in (0, 2)
                ]
                down = [
                    jnp.where(low, pltpu.roll(tails[j], 4, 0), tails[j + 1]) for j in (0, 2)
                ]
                row_send[0, f, part * 3 + quad] = jnp.concatenate(up, 0).astype(jnp.bfloat16)
                row_send[1, f, part * 3 + quad] = jnp.concatenate(down, 0).astype(jnp.bfloat16)

    tall = 1 + (y > 0).astype(jnp.int32) + (y < n_fy - 1).astype(jnp.int32)
    wide = 1 + (x > 0).astype(jnp.int32) + (x < n_fx - 1).astype(jnp.int32)
    pl.semaphore_wait(barrier, tall * wide - 1)
    start((0, 1))

    groups = levels // GROUP
    packed = jnp.zeros((64 * groups, 256), jnp.float32)
    for k in range(GROUP):
        cells = jnp.concatenate(
            [
                jnp.concatenate([fields[f, g * GROUP + k] for g in range(groups)], axis=0)
                for f in range(5)
            ],
            axis=1,
        ).astype(jnp.bfloat16)
        packed += jnp.dot(cells, pick[k], preferred_element_type=jnp.float32)
    for g in range(groups):
        for d in range(2):
            block = packed[64 * g : 64 * g + 64, 128 * d : 128 * d + 128]
            col_send[d, g] = block.astype(jnp.bfloat16)
            ends = jnp.where(low, block[0:8], block[56:64])
            corner_send[d, g] = jnp.concatenate(
                [ends, jnp.zeros_like(ends)], axis=0
            ).astype(jnp.bfloat16)

    start(range(2, 8))
    arrive((0, 1))

    @pl.loop(0, levels // 4)
    def _(quad):
        for f in range(5):
            below = row_recv[0, f, quad].astype(jnp.float32)
            above = row_recv[1, f, quad].astype(jnp.float32)
            for j in range(4):
                b = below[8 * (j // 2) : 8 * (j // 2) + 8]
                a = above[8 * (j // 2) : 8 * (j // 2) + 8]
                if j % 2:
                    b = pltpu.roll(b, 4, 0)
                else:
                    a = pltpu.roll(a, 4, 0)
                row_out[f, quad * 4 + j] = jnp.where(low, b, a)

    arrive(range(2, 8))

    @pl.loop(0, levels // GROUP)
    def _(group):
        for d in range(2):
            col_out[d, group, 0:64] = col_recv[d, group].astype(jnp.float32)
            below = corner_recv[2 * d, group].astype(jnp.float32)[0:8]
            above = corner_recv[2 * d + 1, group].astype(jnp.float32)[0:8]
            col_out[d, group, 64:72] = jnp.where(low, below, above)

    for dy, dx, _, copy in copies(range(8)):

        @pl.when(inside(dy, dx))
        def _():
            copy.wait_send()


def halos(mesh_sizes, tracers, stream):
    n_fy, n_fx = mesh_sizes
    levels = stream.shape[0]
    groups = levels // GROUP
    parts = levels // (2 * GROUP)
    bf16 = jnp.bfloat16
    return pl.pallas_call(
        functools.partial(halo_kernel, n_fy, n_fx),
        out_shape=(
            jax.ShapeDtypeStruct((5, levels, 8, 128), jnp.float32),
            jax.ShapeDtypeStruct((2, groups, 72, 128), jnp.float32),
        ),
        in_specs=[pl.BlockSpec(memory_space=pl.ANY)] * 2,
        out_specs=(pl.BlockSpec(memory_space=pltpu.VMEM),) * 2,
        scratch_shapes=[
            pltpu.VMEM((5, levels, 64, 128), jnp.float32),
            pltpu.VMEM((2, 5, levels // 4, 16, 128), bf16),
            pltpu.VMEM((2, 5, levels // 4, 16, 128), bf16),
            pltpu.VMEM((2, groups, 64, 128), bf16),
            pltpu.VMEM((2, groups, 64, 128), bf16),
            pltpu.VMEM((2, groups, 16, 128), bf16),
            pltpu.VMEM((4, groups, 16, 128), bf16),
            pltpu.VMEM((GROUP, 640, 256), bf16),
            pltpu.SemaphoreType.DMA((2, parts)),
            pltpu.SemaphoreType.DMA((8,)),
            pltpu.SemaphoreType.DMA((8,)),
        ],
        compiler_params=pltpu.CompilerParams(
            collective_id=0, has_side_effects=True, vmem_limit_bytes=60 << 20
        ),
        name="halo_exchange",
    )(tracers, stream)


SPAN = 249
GUARD = 96


def roll(cells, shift, axis):
    return pltpu.roll(cells, shift % cells.shape[axis], axis) if shift else cells


def keep_rows(tiles, buffer, base):
    for i, tile in enumerate([tiles[8], *tiles, tiles[0]]):
        buffer[pl.ds(pl.multiple_of(base + 8 * i, 8), 8), :] = tile


def around(cells, buffer, base):
    buffer[pl.ds(pl.multiple_of(base, 8), 88), :] = jnp.concatenate(
        [cells[64:72], cells, cells[0:8]], axis=0
    )
    return buffer[pl.ds(base + 7, 72), :], buffer[pl.ds(base + 9, 72), :]


def stencil(stream, keep, first, second, base):
    left = stream + roll(stream, 1, 1)
    right = stream + roll(stream, -1, 1)
    left_before, left_after = around(left, first, base)
    right_before, right_after = around(right, second, base)
    corner, below = (left + left_before) * 0.25, (left + left_after) * 0.25
    corner_east, below_east = (right + right_before) * 0.25, (right + right_after) * 0.25
    west = corner - below
    east = corner_east - below_east
    north = corner_east - corner
    south = below_east - below
    centre = (
        1.0
        - jnp.maximum(east, 0.0)
        + jnp.minimum(west, 0.0)
        - jnp.maximum(south, 0.0)
        + jnp.minimum(north, 0.0)
    )
    return tuple(
        jnp.where(keep, w, 0.0)
        for w in (
            centre,
            jnp.maximum(west, 0.0),
            -jnp.minimum(east, 0.0),
            jnp.maximum(north, 0.0),
            -jnp.minimum(south, 0.0),
        )
    )


def advance(tile, weights, buffer, at):
    centre, west, east, north, south = weights
    return (
        centre * tile
        + (west * roll(tile, 1, 1) + east * roll(tile, -1, 1))
        + (north * buffer[pl.ds(at - 1, 8), :] + south * buffer[pl.ds(at + 1, 8), :])
    )


def halves(cells):
    top = cells.astype(jnp.bfloat16)
    return [top, (cells - top.astype(jnp.float32)).astype(jnp.bfloat16)]


def tiles_of(cells):
    return [cells[8 * i : 8 * i + 8] for i in range(cells.shape[0] // 8)]


def column_kernel(
    n_fy,
    n_fx,
    tr_hbm,
    st_hbm,
    row_halo,
    col_halo,
    land,
    convect,
    label,
    w_in_raw,
    w_hid_hbm,
    w_out_raw,
    b_hid,
    b_out,
    out_hbm,
    loss,
    state,
    stream,
    by_row,
    back_rows,
    feats,
    w_in,
    w_hid,
    w_out,
    bias_rows,
    bias,
    place,
    place_local,
    place_ends,
    placing,
    pos,
    offs_v,
    offs,
    *rest,
):
    y = lax.axis_index("fy")
    x = lax.axis_index("fx")
    buffers = (rest[0:5], rest[5:10])
    load_sem, weight_sem, out_sem = rest[10:]
    levels = st_hbm.shape[0]
    parts = 10
    per = levels // parts
    nf = 4 * levels
    f32, bf16 = jnp.float32, jnp.bfloat16

    def loads(part):
        span = pl.ds(part * per, per)
        return (
            pltpu.make_async_copy(tr_hbm.at[:, span], state.at[:, span], load_sem.at[0, part]),
            pltpu.make_async_copy(st_hbm.at[span], stream.at[span], load_sem.at[1, part]),
        )

    for part in range(parts):
        for copy in loads(part):
            copy.start()
    hidden_copy = pltpu.make_async_copy(w_hid_hbm, w_hid, weight_sem.at[0])
    hidden_copy.start()

    w_out[...] = jnp.zeros(w_out.shape, bf16)
    w_out[0 : w_in_raw.shape[0], :] = w_in_raw[...]
    w_in[...] = w_out[...].astype(f32).T.astype(bf16)
    w_out[240:256, :] = jnp.zeros((16, 512), bf16)
    w_out[0 : w_out_raw.shape[0], :] = w_out_raw[...]
    bias_rows[...] = jnp.zeros(bias_rows.shape, f32)
    bias_rows[0:7, :] = b_hid[...]
    bias_rows[7:8, 0 : b_out.shape[1]] = b_out[...]
    bias[...] = bias_rows[...].T

    def iotas(shape):
        return [lax.broadcasted_iota(jnp.int32, shape, d) for d in (0, 1)]

    ones = convect[...].astype(f32)
    r, c = iotas((128, 128))
    upto = jnp.dot(ones, (r <= c).astype(f32), preferred_element_type=f32)
    totals = jnp.broadcast_to(jnp.sum(ones, axis=1, keepdims=True), (64, 128))
    r, c = iotas((72, 64))
    before = jnp.dot((r > c).astype(f32), totals, preferred_element_type=f32)
    pos[...] = jnp.where(convect[...] > 0, (before[0:64] + upto).astype(jnp.int32) - 1, -1)
    offs_v[...] = before.astype(jnp.int32)
    offs_copy = pltpu.make_async_copy(offs_v, offs, weight_sem.at[1])
    offs_copy.start()

    r, c = iotas((256, 256))
    side = r // 128
    for k in range(GROUP):
        j = r % 128 - k * STEP
        f, col = j // 4, j % 4
        good = (j >= 0) & (j < STEP)
        lane_at = 4 + 20 * side + col
        tracer = (f < 4) & (c == 32 * f + lane_at)
        psi = (f == 4) & (c >= 128) & (c % 32 == lane_at)
        place[k] = jnp.where(good & (tracer | psi), 1.0, 0.0).astype(bf16)

    row, lane = iotas((72, 128))
    row_ok = (
        (row < 64)
        | ((row < 68) & (y < n_fy - 1))
        | ((row >= 68) & (y > 0))
    )
    k32 = lane % 32
    middle = (k32 >= 8) & (k32 < 24)
    strip_ok = row_ok & (middle | (k32 < 8) & (x > 0) | (k32 >= 24) & (x < n_fx - 1))

    r, c = iotas((1280, 256))
    k = c % 32
    source = jnp.where(k < 16, k - 8, k + 104)
    owner = jnp.where(c < 128, c // 32, 4)
    good = (k >= 8) & (k < 24) & (r // 256 == owner) & (r % 128 == source)
    place_local[...] = jnp.where(good, 1.0, 0.0).astype(bf16)
    r, c = iotas((256, 512))
    k = c % 128
    source = 32 * (c // 128) + jnp.where(k < 4, k + 8, k - 104)
    good = ((k < 4) | (k >= 124)) & (r % 128 == source)
    place_ends[...] = jnp.where(good, 1.0, 0.0).astype(bf16)
    edge = (lane[0:64] < 4) | (lane[0:64] >= 124)

    @pl.loop(0, levels)
    def _(level):
        @pl.when(level % per == 0)
        def _():
            for copy in loads(level // per):
                copy.wait()

        base = (level % 2) * GUARD
        group = level // GROUP
        packed = jnp.concatenate([col_halo[0, group], col_halo[1, group]], axis=1).astype(bf16)
        beside = jnp.dot(packed, place[level % GROUP], preferred_element_type=f32)

        psi = jnp.concatenate([stream[level], row_halo[4, level]], axis=0)
        cells = [
            jnp.concatenate([state[f, level], row_halo[f, level]], axis=0) for f in range(4)
        ]
        split = jnp.concatenate([part for a in (*cells, psi) for part in halves(a)], axis=1)
        beside += jnp.dot(split, place_local[...], preferred_element_type=f32)
        strip = beside[:, 0:128]
        strip_weights = stencil(
            beside[:, 128:], strip_ok, buffers[1][4], buffers[1][3], base
        )
        main_weights = stencil(psi, row_ok, buffers[1][0], buffers[1][1], base)

        fields = [tiles_of(c) for c in cells] + [tiles_of(strip)]
        main_tiles = list(zip(*map(tiles_of, main_weights)))
        strip_tiles = list(zip(*map(tiles_of, strip_weights)))
        for substep in range(SUBSTEPS):
            held = buffers[substep % 2]
            for f in range(5):
                keep_rows(fields[f], held[f], base)
            count = 9 if substep < SUBSTEPS - 1 else 8
            for i in range(count):
                for f in range(5):
                    fields[f][i] = advance(
                        fields[f][i],
                        main_tiles[i] if f < 4 else strip_tiles[i],
                        held[f],
                        base + 8 + 8 * i,
                    )
        cells = [jnp.concatenate(tiles[0:8], axis=0) for tiles in fields]
        ends = jnp.dot(
            jnp.concatenate(halves(cells[4]), axis=1),
            place_ends[...],
            preferred_element_type=f32,
        )
        for f in range(4):
            done = jnp.where(edge, ends[:, 128 * f : 128 * f + 128], cells[f])
            state[f, level] = done
            by_row[pl.ds(f * levels + level, 64, stride=SPAN), :] = done

    offs_copy.wait()
    hidden_copy.wait()

    slot, _ = iotas((WINDOW, CHUNK))

    def window(i):
        return pl.multiple_of((offs[i, 0] // 128) * 128, 128)

    feats[:, 0:128] = jnp.zeros((256, 128), bf16)
    tail_row, _ = iotas((256 - nf, CHUNK))

    @pl.loop(0, 8)
    def _(j):
        moved = []
        for q in range(8):
            i = j * 8 + q
            picked = by_row[pl.ds(i * SPAN, nf), :]
            on_land = 4.0 * land[pl.ds(i, 1), :].astype(f32)
            tail = jnp.where(tail_row == 0, on_land, 0.0)
            chunk = jnp.concatenate([picked, tail], axis=0).astype(bf16)
            hot = jnp.where(slot == pos[pl.ds(i, 1), :] - window(i), 1.0, 0.0).astype(bf16)
            placing[i] = hot
            moved.append(
                lax.dot_general(
                    chunk, hot, (((1,), (1,)), ((), ())), preferred_element_type=f32
                ).astype(bf16)
            )
        for q in range(8):
            at = window(j * 8 + q)
            feats[:, pl.ds(at, 128)] = feats[:, pl.ds(at, 128)] + moved[q][:, 0:128]
            feats[:, pl.ds(at + 128, 128)] = moved[q][:, 128:]

    def layer(w, inputs, b):
        summed = jnp.dot(w, inputs, preferred_element_type=f32) + b
        return jnp.maximum(summed, 0.15 * summed).astype(bf16)

    @pl.loop(0, (offs[64, 0] + TILE - 1) // TILE)
    def _(t):
        cols = pl.ds(pl.multiple_of(t * TILE, TILE), TILE)
        hidden = layer(w_in[...], feats[:, cols], bias[:, 0:1])
        for l in range(w_hid.shape[0]):
            hidden = layer(w_hid[l], hidden, bias[:, l + 1 : l + 2])
        feats[:, cols] = (
            jnp.dot(w_out[...], hidden, preferred_element_type=f32) + bias[0:256, 7:8]
        ).astype(bf16)

    def out_copy(j):
        rows = pl.ds(pl.multiple_of(j * 8, 8), 8)
        return pltpu.make_async_copy(
            state.at[:, :, rows], out_hbm.at[:, :, rows], out_sem.at[j]
        )

    regime, _ = iotas((8, 8 * 128))

    @pl.loop(0, 8)
    def _(j):
        start = (j % 2) * (8 * SPAN)
        evidence = []
        for q in range(8):
            i = j * 8 + q
            back = jnp.dot(
                feats[:, pl.ds(window(i), WINDOW)], placing[i], preferred_element_type=f32
            )
            back_rows[pl.ds(start + q * SPAN, nf), :] = back[0:nf]
            evidence.append(back[nf : nf + 8])
        rows = pl.ds(pl.multiple_of(j * 8, 8), 8)
        for f in range(4):
            for level in range(levels):
                state[f, level, rows] = (
                    state[f, level, rows]
                    + back_rows[pl.ds(start + f * levels + level, 8, stride=SPAN), :]
                )
        out_copy(j).start()
        evidence = jnp.concatenate(evidence, axis=1)
        alpha = 1.0 + (jnp.maximum(evidence, 0.0) + jnp.log1p(jnp.exp(-jnp.abs(evidence))))
        alpha = jnp.where(regime < 4, alpha, 0.0)
        strength = jnp.sum(alpha, axis=0, keepdims=True)
        labels = jnp.concatenate([label[pl.ds(j * 8 + q, 1), :] for q in range(8)], axis=1)
        chosen = jnp.sum(jnp.where(regime == labels, alpha, 0.0), axis=0, keepdims=True)
        value = jnp.log(strength) - jnp.log(chosen)
        for q in range(8):
            at = pl.ds(j * 8 + q, 1)
            loss[at, :] = jnp.where(
                convect[at, :] > 0, value[:, q * 128 : q * 128 + 128], 0.0
            )

    @pl.loop(0, 8)
    def _(j):
        out_copy(j).wait()


def columns(mesh_sizes, *operands):
    n_fy, n_fx = mesh_sizes
    tracers, stream = operands[0], operands[1]
    any_space = pl.BlockSpec(memory_space=pl.ANY)
    vmem = pl.BlockSpec(memory_space=pltpu.VMEM)
    f32, bf16 = jnp.float32, jnp.bfloat16
    return pl.pallas_call(
        functools.partial(column_kernel, n_fy, n_fx),
        out_shape=(
            jax.ShapeDtypeStruct(tracers.shape, f32),
            jax.ShapeDtypeStruct((64, 128), f32),
        ),
        in_specs=[any_space] * 2 + [vmem] * 6 + [any_space] + [vmem] * 3,
        out_specs=(any_space, vmem),
        scratch_shapes=[
            pltpu.VMEM(tracers.shape, f32),
            pltpu.VMEM(stream.shape, f32),
            pltpu.VMEM((64 * SPAN, 128), f32),
            pltpu.VMEM((16 * SPAN, 128), f32),
            pltpu.VMEM((256, MOST + 512), bf16),
            pltpu.VMEM((512, 256), bf16),
            pltpu.VMEM((6, 512, 512), bf16),
            pltpu.VMEM((256, 512), bf16),
            pltpu.VMEM((128, 512), f32),
            pltpu.VMEM((512, 128), f32),
            pltpu.VMEM((GROUP, 256, 256), bf16),
            pltpu.VMEM((1280, 256), bf16),
            pltpu.VMEM((256, 512), bf16),
            pltpu.VMEM((64, WINDOW, CHUNK), bf16),
            pltpu.VMEM((64, 128), jnp.int32),
            pltpu.VMEM((72, 128), jnp.int32),
            pltpu.SMEM((72, 128), jnp.int32),
        ]
        + [pltpu.VMEM((2 * GUARD, 128), f32)] * 10
        + [
            pltpu.SemaphoreType.DMA((2, 10)),
            pltpu.SemaphoreType.DMA((2,)),
            pltpu.SemaphoreType.DMA((8,)),
        ],
        compiler_params=pltpu.CompilerParams(vmem_limit_bytes=60 << 20),
        name="transport_and_network",
    )(*operands)


def body(sizes, tracers, stream, land, convect, label, w_in, w_hid, b_hid, w_out, b_out):
    row_halo, col_halo = halos(sizes, tracers, stream)
    return columns(
        sizes,
        tracers,
        stream,
        row_halo,
        col_halo,
        land,
        convect,
        label,
        w_in.T,
        w_hid,
        w_out,
        b_hid,
        b_out.reshape(1, -1),
    )


def solution(mesh):
    placed = (
        P(None, None, "fy", "fx"),
        P(None, "fy", "fx"),
        P("fy", "fx"),
        P("fy", "fx"),
        P("fy", "fx"),
        P(),
        P(),
        P(),
        P(),
        P(),
    )
    sizes = (mesh.shape["fy"], mesh.shape["fx"])
    return jax.shard_map(
        functools.partial(body, sizes),
        mesh=mesh,
        in_specs=placed,
        out_specs=(P(None, None, "fy", "fx"), P("fy", "fx")),
        check_vma=False,
    )
```

```python
import functools

import jax
import jax.numpy as jnp
from jax import lax
from jax.experimental import pallas as pl
from jax.experimental.pallas import tpu as pltpu
from jax.sharding import PartitionSpec as P

SUBSTEPS = 4
MESH = pl.DeviceIdType.MESH
CHUNK = 128
WINDOW = 256
TILE = 2048
MOST = 4096
GROUP = 6
STEP = 20

WAYS = ((-1, 0), (1, 0), (0, 1), (0, -1), (-1, 1), (1, 1), (-1, -1), (1, -1))


def halo_kernel(
    n_fy,
    n_fx,
    tr_hbm,
    st_hbm,
    row_out,
    col_out,
    fields,
    row_send,
    row_recv,
    col_send,
    col_recv,
    corner_send,
    corner_recv,
    pick,
    load_sem,
    send_sem,
    recv_sem,
):
    y = lax.axis_index("fy")
    x = lax.axis_index("fx")
    levels = st_hbm.shape[0]
    per = 2 * GROUP
    parts = levels // per

    def inside(dy, dx):
        ok_y = (y + dy >= 0) & (y + dy < n_fy)
        ok_x = (x + dx >= 0) & (x + dx < n_fx)
        return ok_y & ok_x

    barrier = pltpu.get_barrier_semaphore()
    for dy, dx in WAYS:

        @pl.when(inside(dy, dx))
        def _():
            pl.semaphore_signal(barrier, inc=1, device_id=(x + dx, y + dy), device_id_type=MESH)

    def loads(part):
        span = pl.ds(part * per, per)
        return (
            pltpu.make_async_copy(
                tr_hbm.at[:, span], fields.at[pl.ds(0, 4), span], load_sem.at[0, part]
            ),
            pltpu.make_async_copy(st_hbm.at[span], fields.at[4, span], load_sem.at[1, part]),
        )

    for part in range(parts):
        for copy in loads(part):
            copy.start()

    r = lax.broadcasted_iota(jnp.int32, (640, 256), 0)
    c = lax.broadcasted_iota(jnp.int32, (640, 256), 1)
    col = r % 128 - jnp.where(c < 128, 124, 0)
    at = jnp.where((col >= 0) & (col < 4), c % 128 - 4 * (r // 128) - col, -1)
    for k in range(GROUP):
        pick[k] = jnp.where(at == k * STEP, 1.0, 0.0).astype(jnp.bfloat16)

    low = lax.broadcasted_iota(jnp.int32, (8, 128), 0) < 4

    def copies(ways):
        for way in ways:
            dy, dx = WAYS[way]
            if way < 2:
                src, dst = row_send.at[way], row_recv.at[way]
            elif way < 4:
                src, dst = col_send.at[way - 2], col_recv.at[way - 2]
            else:
                src, dst = corner_send.at[(way - 4) // 2], corner_recv.at[way - 4]
            yield dy, dx, dst, pltpu.make_async_remote_copy(
                src_ref=src,
                dst_ref=dst,
                send_sem=send_sem.at[way],
                recv_sem=recv_sem.at[way],
                device_id=(x + dx, y + dy),
                device_id_type=MESH,
            )

    def start(ways):
        for dy, dx, _, copy in copies(ways):

            @pl.when(inside(dy, dx))
            def _():
                copy.start()

    def arrive(ways):
        for dy, dx, dst, copy in copies(ways):

            @pl.when(inside(-dy, -dx))
            def _():
                copy.wait_recv()

            @pl.when(jnp.logical_not(inside(-dy, -dx)))
            def _():
                dst[...] = jnp.zeros(dst.shape, dst.dtype)

    @pl.loop(0, parts)
    def _(part):
        for copy in loads(part):
            copy.wait()
        first = part * per
        for quad in range(per // 4):
            for f in range(5):
                heads = [fields[f, first + quad * 4 + j, 0:8] for j in range(4)]
                tails = [fields[f, first + quad * 4 + j, 56:64] for j in range(4)]
                up = [
                    jnp.where(low, heads[j], pltpu.roll(heads[j + 1], 4, 0)) for j in (0, 2)
                ]
                down = [
                    jnp.where(low, pltpu.roll(tails[j], 4, 0), tails[j + 1]) for j in (0, 2)
                ]
                row_send[0, f, part * 3 + quad] = jnp.concatenate(up, 0).astype(jnp.bfloat16)
                row_send[1, f, part * 3 + quad] = jnp.concatenate(down, 0).astype(jnp.bfloat16)

    tall = 1 + (y > 0).astype(jnp.int32) + (y < n_fy - 1).astype(jnp.int32)
    wide = 1 + (x > 0).astype(jnp.int32) + (x < n_fx - 1).astype(jnp.int32)
    pl.semaphore_wait(barrier, tall * wide - 1)
    start((0, 1))

    groups = levels // GROUP
    packed = jnp.zeros((64 * groups, 256), jnp.float32)
    for k in range(GROUP):
        cells = jnp.concatenate(
            [
                jnp.concatenate([fields[f, g * GROUP + k] for g in range(groups)], axis=0)
                for f in range(5)
            ],
            axis=1,
        ).astype(jnp.bfloat16)
        packed += jnp.dot(cells, pick[k], preferred_element_type=jnp.float32)
    for g in range(groups):
        for d in range(2):
            block = packed[64 * g : 64 * g + 64, 128 * d : 128 * d + 128]
            col_send[d, g] = block.astype(jnp.bfloat16)
            ends = jnp.where(low, block[0:8], block[56:64])
            corner_send[d, g] = jnp.concatenate(
                [ends, jnp.zeros_like(ends)], axis=0
            ).astype(jnp.bfloat16)

    start(range(2, 8))
    arrive((0, 1))

    @pl.loop(0, levels // 4)
    def _(quad):
        for f in range(5):
            below = row_recv[0, f, quad].astype(jnp.float32)
            above = row_recv[1, f, quad].astype(jnp.float32)
            for j in range(4):
                b = below[8 * (j // 2) : 8 * (j // 2) + 8]
                a = above[8 * (j // 2) : 8 * (j // 2) + 8]
                if j % 2:
                    b = pltpu.roll(b, 4, 0)
                else:
                    a = pltpu.roll(a, 4, 0)
                row_out[f, quad * 4 + j] = jnp.where(low, b, a)

    arrive(range(2, 8))

    @pl.loop(0, levels // GROUP)
    def _(group):
        for d in range(2):
            col_out[d, group, 0:64] = col_recv[d, group].astype(jnp.float32)
            below = corner_recv[2 * d, group].astype(jnp.float32)[0:8]
            above = corner_recv[2 * d + 1, group].astype(jnp.float32)[0:8]
            col_out[d, group, 64:72] = jnp.where(low, below, above)

    for dy, dx, _, copy in copies(range(8)):

        @pl.when(inside(dy, dx))
        def _():
            copy.wait_send()


def halos(mesh_sizes, tracers, stream):
    n_fy, n_fx = mesh_sizes
    levels = stream.shape[0]
    groups = levels // GROUP
    parts = levels // (2 * GROUP)
    bf16 = jnp.bfloat16
    return pl.pallas_call(
        functools.partial(halo_kernel, n_fy, n_fx),
        out_shape=(
            jax.ShapeDtypeStruct((5, levels, 8, 128), jnp.float32),
            jax.ShapeDtypeStruct((2, groups, 72, 128), jnp.float32),
        ),
        in_specs=[pl.BlockSpec(memory_space=pl.ANY)] * 2,
        out_specs=(pl.BlockSpec(memory_space=pltpu.VMEM),) * 2,
        scratch_shapes=[
            pltpu.VMEM((5, levels, 64, 128), jnp.float32),
            pltpu.VMEM((2, 5, levels // 4, 16, 128), bf16),
            pltpu.VMEM((2, 5, levels // 4, 16, 128), bf16),
            pltpu.VMEM((2, groups, 64, 128), bf16),
            pltpu.VMEM((2, groups, 64, 128), bf16),
            pltpu.VMEM((2, groups, 16, 128), bf16),
            pltpu.VMEM((4, groups, 16, 128), bf16),
            pltpu.VMEM((GROUP, 640, 256), bf16),
            pltpu.SemaphoreType.DMA((2, parts)),
            pltpu.SemaphoreType.DMA((8,)),
            pltpu.SemaphoreType.DMA((8,)),
        ],
        compiler_params=pltpu.CompilerParams(
            collective_id=0, has_side_effects=True, vmem_limit_bytes=60 << 20
        ),
        name="halo_exchange",
    )(tracers, stream)


SPAN = 249
GUARD = 96


def roll(cells, shift, axis):
    return pltpu.roll(cells, shift % cells.shape[axis], axis) if shift else cells


def keep_rows(tiles, buffer, base):
    for i, tile in enumerate([tiles[8], *tiles, tiles[0]]):
        buffer[pl.ds(pl.multiple_of(base + 8 * i, 8), 8), :] = tile


def around(cells, buffer, base):
    buffer[pl.ds(pl.multiple_of(base, 8), 88), :] = jnp.concatenate(
        [cells[64:72], cells, cells[0:8]], axis=0
    )
    return buffer[pl.ds(base + 7, 72), :], buffer[pl.ds(base + 9, 72), :]


def stencil(stream, keep, first, second, base):
    left = stream + roll(stream, 1, 1)
    right = stream + roll(stream, -1, 1)
    left_before, left_after = around(left, first, base)
    right_before, right_after = around(right, second, base)
    corner, below = (left + left_before) * 0.25, (left + left_after) * 0.25
    corner_east, below_east = (right + right_before) * 0.25, (right + right_after) * 0.25
    west = corner - below
    east = corner_east - below_east
    north = corner_east - corner
    south = below_east - below
    centre = (
        1.0
        - jnp.maximum(east, 0.0)
        + jnp.minimum(west, 0.0)
        - jnp.maximum(south, 0.0)
        + jnp.minimum(north, 0.0)
    )
    return tuple(
        jnp.where(keep, w, 0.0)
        for w in (
            centre,
            jnp.maximum(west, 0.0),
            -jnp.minimum(east, 0.0),
            jnp.maximum(north, 0.0),
            -jnp.minimum(south, 0.0),
        )
    )


def advance(tile, weights, buffer, at):
    centre, west, east, north, south = weights
    return (
        centre * tile
        + (west * roll(tile, 1, 1) + east * roll(tile, -1, 1))
        + (north * buffer[pl.ds(at - 1, 8), :] + south * buffer[pl.ds(at + 1, 8), :])
    )


def halves(cells):
    top = cells.astype(jnp.bfloat16)
    return [top, (cells - top.astype(jnp.float32)).astype(jnp.bfloat16)]


def tiles_of(cells):
    return [cells[8 * i : 8 * i + 8] for i in range(cells.shape[0] // 8)]


def column_kernel(
    n_fy,
    n_fx,
    tr_hbm,
    st_hbm,
    row_halo,
    col_halo,
    land,
    convect,
    label,
    w_in_raw,
    w_hid_hbm,
    w_out_raw,
    b_hid,
    b_out,
    out_hbm,
    loss,
    state,
    stream,
    by_row,
    back_rows,
    feats,
    w_in,
    w_hid,
    w_out,
    bias_rows,
    bias,
    place,
    place_local,
    place_ends,
    placing,
    pos,
    offs_v,
    offs,
    *rest,
):
    y = lax.axis_index("fy")
    x = lax.axis_index("fx")
    buffers = (rest[0:5], rest[5:10])
    load_sem, weight_sem, out_sem = rest[10:]
    levels = st_hbm.shape[0]
    parts = 10
    per = levels // parts
    nf = 4 * levels
    f32, bf16 = jnp.float32, jnp.bfloat16

    def loads(part):
        span = pl.ds(part * per, per)
        return (
            pltpu.make_async_copy(tr_hbm.at[:, span], state.at[:, span], load_sem.at[0, part]),
            pltpu.make_async_copy(st_hbm.at[span], stream.at[span], load_sem.at[1, part]),
        )

    for part in range(parts):
        for copy in loads(part):
            copy.start()
    hidden_copy = pltpu.make_async_copy(w_hid_hbm, w_hid, weight_sem.at[0])
    hidden_copy.start()

    w_out[...] = jnp.zeros(w_out.shape, bf16)
    w_out[0 : w_in_raw.shape[0], :] = w_in_raw[...]
    w_in[...] = w_out[...].astype(f32).T.astype(bf16)
    w_out[240:256, :] = jnp.zeros((16, 512), bf16)
    w_out[0 : w_out_raw.shape[0], :] = w_out_raw[...]
    bias_rows[...] = jnp.zeros(bias_rows.shape, f32)
    bias_rows[0:7, :] = b_hid[...]
    bias_rows[7:8, 0 : b_out.shape[1]] = b_out[...]
    bias[...] = bias_rows[...].T

    def iotas(shape):
        return [lax.broadcasted_iota(jnp.int32, shape, d) for d in (0, 1)]

    ones = convect[...].astype(f32)
    r, c = iotas((128, 128))
    upto = jnp.dot(ones, (r <= c).astype(f32), preferred_element_type=f32)
    totals = jnp.broadcast_to(jnp.sum(ones, axis=1, keepdims=True), (64, 128))
    r, c = iotas((72, 64))
    before = jnp.dot((r > c).astype(f32), totals, preferred_element_type=f32)
    pos[...] = jnp.where(convect[...] > 0, (before[0:64] + upto).astype(jnp.int32) - 1, -1)
    offs_v[...] = before.astype(jnp.int32)
    offs_copy = pltpu.make_async_copy(offs_v, offs, weight_sem.at[1])
    offs_copy.start()

    r, c = iotas((256, 256))
    side = r // 128
    for k in range(GROUP):
        j = r % 128 - k * STEP
        f, col = j // 4, j % 4
        good = (j >= 0) & (j < STEP)
        lane_at = 4 + 20 * side + col
        tracer = (f < 4) & (c == 32 * f + lane_at)
        psi = (f == 4) & (c >= 128) & (c % 32 == lane_at)
        place[k] = jnp.where(good & (tracer | psi), 1.0, 0.0).astype(bf16)

    row, lane = iotas((72, 128))
    row_ok = (
        (row < 64)
        | ((row < 68) & (y < n_fy - 1))
        | ((row >= 68) & (y > 0))
    )
    k32 = lane % 32
    middle = (k32 >= 8) & (k32 < 24)
    strip_ok = row_ok & (middle | (k32 < 8) & (x > 0) | (k32 >= 24) & (x < n_fx - 1))

    r, c = iotas((1280, 256))
    k = c % 32
    source = jnp.where(k < 16, k - 8, k + 104)
    owner = jnp.where(c < 128, c // 32, 4)
    good = (k >= 8) & (k < 24) & (r // 256 == owner) & (r % 128 == source)
    place_local[...] = jnp.where(good, 1.0, 0.0).astype(bf16)
    r, c = iotas((256, 512))
    k = c % 128
    source = 32 * (c // 128) + jnp.where(k < 4, k + 8, k - 104)
    good = ((k < 4) | (k >= 124)) & (r % 128 == source)
    place_ends[...] = jnp.where(good, 1.0, 0.0).astype(bf16)
    edge = (lane[0:64] < 4) | (lane[0:64] >= 124)

    @pl.loop(0, levels)
    def _(level):
        @pl.when(level % per == 0)
        def _():
            for copy in loads(level // per):
                copy.wait()

        base = (level % 2) * GUARD
        group = level // GROUP
        packed = jnp.concatenate([col_halo[0, group], col_halo[1, group]], axis=1).astype(bf16)
        beside = jnp.dot(packed, place[level % GROUP], preferred_element_type=f32)

        psi = jnp.concatenate([stream[level], row_halo[4, level]], axis=0)
        cells = [
            jnp.concatenate([state[f, level], row_halo[f, level]], axis=0) for f in range(4)
        ]
        split = jnp.concatenate([part for a in (*cells, psi) for part in halves(a)], axis=1)
        beside += jnp.dot(split, place_local[...], preferred_element_type=f32)
        strip = beside[:, 0:128]
        strip_weights = stencil(
            beside[:, 128:], strip_ok, buffers[1][4], buffers[1][3], base
        )
        main_weights = stencil(psi, row_ok, buffers[1][0], buffers[1][1], base)

        fields = [tiles_of(c) for c in cells] + [tiles_of(strip)]
        main_tiles = list(zip(*map(tiles_of, main_weights)))
        strip_tiles = list(zip(*map(tiles_of, strip_weights)))
        for substep in range(SUBSTEPS):
            held = buffers[substep % 2]
            for f in range(5):
                keep_rows(fields[f], held[f], base)
            count = 9 if substep < SUBSTEPS - 1 else 8
            for i in range(count):
                for f in range(5):
                    fields[f][i] = advance(
                        fields[f][i],
                        main_tiles[i] if f < 4 else strip_tiles[i],
                        held[f],
                        base + 8 + 8 * i,
                    )
        cells = [jnp.concatenate(tiles[0:8], axis=0) for tiles in fields]
        ends = jnp.dot(
            jnp.concatenate(halves(cells[4]), axis=1),
            place_ends[...],
            preferred_element_type=f32,
        )
        for f in range(4):
            done = jnp.where(edge, ends[:, 128 * f : 128 * f + 128], cells[f])
            state[f, level] = done
            by_row[pl.ds(f * levels + level, 64, stride=SPAN), :] = done

    offs_copy.wait()
    hidden_copy.wait()

    slot, _ = iotas((WINDOW, CHUNK))

    def window(i):
        return pl.multiple_of((offs[i, 0] // 128) * 128, 128)

    feats[:, 0:128] = jnp.zeros((256, 128), bf16)
    tail_row, _ = iotas((256 - nf, CHUNK))

    @pl.loop(0, 8)
    def _(j):
        moved = []
        for q in range(8):
            i = j * 8 + q
            picked = by_row[pl.ds(i * SPAN, nf), :]
            on_land = 4.0 * land[pl.ds(i, 1), :].astype(f32)
            tail = jnp.where(tail_row == 0, on_land, 0.0)
            chunk = jnp.concatenate([picked, tail], axis=0).astype(bf16)
            hot = jnp.where(slot == pos[pl.ds(i, 1), :] - window(i), 1.0, 0.0).astype(bf16)
            placing[i] = hot
            moved.append(
                lax.dot_general(
                    chunk, hot, (((1,), (1,)), ((), ())), preferred_element_type=f32
                ).astype(bf16)
            )
        for q in range(8):
            at = window(j * 8 + q)
            feats[:, pl.ds(at, 128)] = feats[:, pl.ds(at, 128)] + moved[q][:, 0:128]
            feats[:, pl.ds(at + 128, 128)] = moved[q][:, 128:]

    def layer(w, inputs, b):
        summed = jnp.dot(w, inputs, preferred_element_type=f32) + b
        return jnp.maximum(summed, 0.15 * summed).astype(bf16)

    @pl.loop(0, (offs[64, 0] + TILE - 1) // TILE)
    def _(t):
        cols = pl.ds(pl.multiple_of(t * TILE, TILE), TILE)
        hidden = layer(w_in[...], feats[:, cols], bias[:, 0:1])
        for l in range(w_hid.shape[0]):
            hidden = layer(w_hid[l], hidden, bias[:, l + 1 : l + 2])
        feats[:, cols] = (
            jnp.dot(w_out[...], hidden, preferred_element_type=f32) + bias[0:256, 7:8]
        ).astype(bf16)

    def out_copy(j):
        rows = pl.ds(pl.multiple_of(j * 8, 8), 8)
        return pltpu.make_async_copy(
            state.at[:, :, rows], out_hbm.at[:, :, rows], out_sem.at[j]
        )

    regime, _ = iotas((8, 8 * 128))

    @pl.loop(0, 8)
    def _(j):
        start = (j % 2) * (8 * SPAN)
        evidence = []
        for q in range(8):
            i = j * 8 + q
            back = jnp.dot(
                feats[:, pl.ds(window(i), WINDOW)], placing[i], preferred_element_type=f32
            )
            back_rows[pl.ds(start + q * SPAN, nf), :] = back[0:nf]
            evidence.append(back[nf : nf + 8])
        rows = pl.ds(pl.multiple_of(j * 8, 8), 8)
        for f in range(4):
            for level in range(levels):
                state[f, level, rows] = (
                    state[f, level, rows]
                    + back_rows[pl.ds(start + f * levels + level, 8, stride=SPAN), :]
                )
        out_copy(j).start()
        evidence = jnp.concatenate(evidence, axis=1)
        alpha = 1.0 + (jnp.maximum(evidence, 0.0) + jnp.log1p(jnp.exp(-jnp.abs(evidence))))
        alpha = jnp.where(regime < 4, alpha, 0.0)
        strength = jnp.sum(alpha, axis=0, keepdims=True)
        labels = jnp.concatenate([label[pl.ds(j * 8 + q, 1), :] for q in range(8)], axis=1)
        chosen = jnp.sum(jnp.where(regime == labels, alpha, 0.0), axis=0, keepdims=True)
        value = jnp.log(strength) - jnp.log(chosen)
        for q in range(8):
            at = pl.ds(j * 8 + q, 1)
            loss[at, :] = jnp.where(
                convect[at, :] > 0, value[:, q * 128 : q * 128 + 128], 0.0
            )

    @pl.loop(0, 8)
    def _(j):
        out_copy(j).wait()


def columns(mesh_sizes, *operands):
    n_fy, n_fx = mesh_sizes
    tracers, stream = operands[0], operands[1]
    any_space = pl.BlockSpec(memory_space=pl.ANY)
    vmem = pl.BlockSpec(memory_space=pltpu.VMEM)
    f32, bf16 = jnp.float32, jnp.bfloat16
    return pl.pallas_call(
        functools.partial(column_kernel, n_fy, n_fx),
        out_shape=(
            jax.ShapeDtypeStruct(tracers.shape, f32),
            jax.ShapeDtypeStruct((64, 128), f32),
        ),
        in_specs=[any_space] * 2 + [vmem] * 6 + [any_space] + [vmem] * 3,
        out_specs=(any_space, vmem),
        scratch_shapes=[
            pltpu.VMEM(tracers.shape, f32),
            pltpu.VMEM(stream.shape, f32),
            pltpu.VMEM((64 * SPAN, 128), f32),
            pltpu.VMEM((16 * SPAN, 128), f32),
            pltpu.VMEM((256, MOST + 512), bf16),
            pltpu.VMEM((512, 256), bf16),
            pltpu.VMEM((6, 512, 512), bf16),
            pltpu.VMEM((256, 512), bf16),
            pltpu.VMEM((128, 512), f32),
            pltpu.VMEM((512, 128), f32),
            pltpu.VMEM((GROUP, 256, 256), bf16),
            pltpu.VMEM((1280, 256), bf16),
            pltpu.VMEM((256, 512), bf16),
            pltpu.VMEM((64, WINDOW, CHUNK), bf16),
            pltpu.VMEM((64, 128), jnp.int32),
            pltpu.VMEM((72, 128), jnp.int32),
            pltpu.SMEM((72, 128), jnp.int32),
        ]
        + [pltpu.VMEM((2 * GUARD, 128), f32)] * 10
        + [
            pltpu.SemaphoreType.DMA((2, 10)),
            pltpu.SemaphoreType.DMA((2,)),
            pltpu.SemaphoreType.DMA((8,)),
        ],
        compiler_params=pltpu.CompilerParams(vmem_limit_bytes=60 << 20),
        name="transport_and_network",
    )(*operands)


def body(sizes, tracers, stream, land, convect, label, w_in, w_hid, b_hid, w_out, b_out):
    row_halo, col_halo = halos(sizes, tracers, stream)
    return columns(
        sizes,
        tracers,
        stream,
        row_halo,
        col_halo,
        land,
        convect,
        label,
        w_in.T,
        w_hid,
        w_out,
        b_hid,
        b_out.reshape(1, -1),
    )


def solution(mesh):
    placed = (
        P(None, None, "fy", "fx"),
        P(None, "fy", "fx"),
        P("fy", "fx"),
        P("fy", "fx"),
        P("fy", "fx"),
        P(),
        P(),
        P(),
        P(),
        P(),
    )
    sizes = (mesh.shape["fy"], mesh.shape["fx"])
    return jax.shard_map(
        functools.partial(body, sizes),
        mesh=mesh,
        in_specs=placed,
        out_specs=(P(None, None, "fy", "fx"), P("fy", "fx")),
        check_vma=False,
    )
```
